1024 devices in a mesh: rep: 8 (over z), outer: 8 (over y), local: 16 (over x, core).
Axes of the slice: x: 8, y: 8, z: 8, core: 2. Of those that a mesh axis runs over, the one named last changes fastest.
Arguments:
- tokens: bfloat16 [4096, 4096], P(('outer', 'local'), 'rep'), may hold values from -6 to 6
- out_grad: bfloat16 [4096, 4096], P(('outer', 'local'), 'rep'), may hold values from -6 to 6
- expert_ids: int32 [4096, 8], P(('outer', 'local')), may hold values from 0 to 127, all different within a row
- route_weights: float32 [4096, 8], P(('outer', 'local')), may hold values from 0.1 to 1
- gate_weight: bfloat16 [128, 4096, 1024], P(('outer', 'local'), 'rep'), may hold values from -0.09375 to 0.09375
- up_weight: bfloat16 [128, 4096, 1024], P(('outer', 'local'), 'rep'), may hold values from -0.09375 to 0.09375
- down_weight: bfloat16 [128, 1024, 4096], P(('outer', 'local'), None, 'rep'), may hold values from -0.1875 to 0.1875
Outputs:
- x_grad: bfloat16 [4096, 4096], P(('outer', 'local'), 'rep')
The draws below stay inside these ranges and needn't reach their ends.
Inputs may be any that keep to these rules, and one draw needn't show every extreme that they name: `expert_ids`: each token names 8 different experts.
All inputs are finite; a program needn't handle non-finite values.
Results may differ from the reference program's by a relative error of at most 0.0064.
Values may be sent and summed in bfloat16 or wider, within the bound.
No kernel may reach another device: no remote copies, remote signals or barrier semaphores. Data moves between devices by JAX's collectives and lax.ppermute only.
A program may use at most 64 MiB of HBM per device.

```python
import math
import jax
import jax.numpy as jnp
from jax import lax

D = 4096
FF = 1024
TOP = 8
TOK_DEV = 32
EXPERTS = 128
CAP = 4
TOKENS = 4096


def level_of(stream_key, shape, cuts, least, largest):
    factor_of, own = 1.0, jax.random.fold_in(stream_key, 6)
    for dim, parts in cuts:
        draws = jnp.exp(jax.random.uniform(jax.random.fold_in(own, dim), (parts,), jnp.float32, least / len(cuts), largest / len(cuts)))
        factor_of = factor_of * jnp.repeat(draws, shape[dim] // parts).reshape([-1 if axis == dim else 1 for axis in range(len(shape))])
    return factor_of


def distinct(key, rows, number_of, top, lift):
    order = jax.random.permutation(jax.random.fold_in(key, 1), number_of)
    favour = order
    for power in range(3):
        favour = favour * favour // number_of
    favour = favour * lift // number_of
    tickets = jax.random.randint(jax.random.fold_in(key, 2), (rows, number_of), 0, 4096) + favour
    holders = jax.random.permutation(jax.random.fold_in(key, 3), rows)[jnp.arange(number_of) % rows]
    tickets = jnp.where(jnp.arange(rows)[:, None] == holders[None, :], 1 << 14, tickets)
    merit = tickets * number_of + jnp.arange(number_of)
    return lax.top_k(merit.astype(jnp.int32), top)[1].astype(jnp.int32)


def noise(own_key, extent, scale, reach, cuts=(), kind=jnp.bfloat16):
    array = jax.random.normal(own_key, extent, jnp.float32) * scale
    if len(cuts) > 0:
        array = level_of(own_key, extent, cuts, -0.22, 0.18) * array
    return jnp.clip(array, min=-reach, max=reach).astype(kind)


def setup_inputs(seed: int = 0) -> dict:
    key_of = jax.random.split(jax.random.key(seed), 8)
    tokens = noise(key_of[0], (TOKENS, D), 1.0, 6.0, ((0, 128), (1, 8)))
    out_grad = noise(key_of[1], (TOKENS, D), 1.0, 6.0, ((0, 128), (1, 8)))
    expert_ids = distinct(key_of[2], TOKENS, EXPERTS, TOP, 1024)
    route_weights = jnp.clip(jnp.exp(math.log(1.0) - 2.3025851 * jax.random.uniform(key_of[3], (TOKENS, TOP), jnp.float32) ** level_of(key_of[3], (TOKENS, TOP), ((0, 128),), -0.2, 0.2)), 0.1, 1.0)
    gate_weight = noise(key_of[4], (EXPERTS, D, FF), D ** -0.5, 0.09375, ((0, 128), (1, 8)))
    up_weight = noise(key_of[5], (EXPERTS, D, FF), D ** -0.5, 0.09375, ((0, 128), (1, 8)))
    down_weight = noise(key_of[6], (EXPERTS, FF, D), FF ** -0.5, 0.1875, ((0, 128), (2, 8)))
    return dict(tokens=tokens, out_grad=out_grad, expert_ids=expert_ids, route_weights=route_weights, gate_weight=gate_weight, up_weight=up_weight, down_weight=down_weight)


def reference(tokens, out_grad, expert_ids, route_weights, gate_weight, up_weight, down_weight):
    groups = TOKENS // TOK_DEV
    row_count = TOK_DEV * TOP
    expert_list = expert_ids.reshape(groups, row_count)
    onehot = (expert_list[:, :, None] == jnp.arange(EXPERTS, dtype=jnp.int32)[None, None, :]).astype(jnp.int32)
    before = (jnp.cumsum(onehot, axis=1) - onehot).astype(jnp.int32)
    slot_index = jnp.sum(before * onehot, axis=2).astype(jnp.int32)
    placed = (slot_index[:, :, None] == jnp.arange(CAP, dtype=jnp.int32)[None, None, :]).astype(jnp.int32)
    matches = onehot[:, :, :, None] * placed[:, :, None, :]
    valid_flags = jnp.sum(matches, axis=1).astype(jnp.int32)
    positions = jnp.arange(row_count, dtype=jnp.int32)
    source = jnp.sum(matches * positions[None, :, None, None], axis=1).astype(jnp.int32)
    flat_rows = (jnp.arange(groups, dtype=jnp.int32)[:, None, None] * row_count + source).astype(jnp.int32)
    flat_rows = jnp.transpose(flat_rows, (1, 0, 2)).reshape(EXPERTS, groups * CAP)
    valid_flags = jnp.transpose(valid_flags, (1, 0, 2)).reshape(EXPERTS, groups * CAP)
    token_rows = (flat_rows // TOP).astype(jnp.int32)
    scaled = (route_weights[:, :, None] * out_grad.astype(jnp.float32)[:, None, :]).astype(jnp.bfloat16)
    scaled = scaled.reshape(TOKENS * TOP, D)

    def one_expert(carry_sum, inputs):
        token_index, row_index, keep_flags, w_gate, w_up, w_down = inputs
        keep_mask = keep_flags[:, None] > 0
        zero_value = jnp.zeros((), jnp.bfloat16)
        x_rows = jnp.where(keep_mask, tokens[token_index], zero_value)
        dy_rows = jnp.where(keep_mask, scaled[row_index], zero_value)
        gate_values = jnp.dot(x_rows, w_gate, preferred_element_type=jnp.float32)
        up_values = jnp.dot(x_rows, w_up, preferred_element_type=jnp.float32)
        hidden_values = jnp.dot(dy_rows, w_down.T, preferred_element_type=jnp.float32)
        gate_sigmoid = jax.nn.sigmoid(gate_values)
        up_rows = (hidden_values * gate_values * gate_sigmoid).astype(jnp.bfloat16)
        gate_rows = (hidden_values * up_values * gate_sigmoid * (1.0 + gate_values * (1.0 - gate_sigmoid))).astype(jnp.bfloat16)
        row_grad = (jnp.dot(gate_rows, w_gate.T, preferred_element_type=jnp.float32)
                    + jnp.dot(up_rows, w_up.T, preferred_element_type=jnp.float32)).astype(jnp.bfloat16)
        carry_sum = carry_sum.at[token_index].add(jnp.where(keep_mask, row_grad.astype(jnp.float32), 0.0))
        return carry_sum, None

    initial = jnp.zeros((TOKENS, D), jnp.float32)
    grad_total, unused = lax.scan(
        one_expert, initial, (token_rows, flat_rows, valid_flags, gate_weight, up_weight, down_weight))
    return grad_total.astype(jnp.bfloat16)
```

```python
import jax
import jax.numpy as jnp
from jax import lax
from jax.experimental import pallas as pl
from jax.experimental.pallas import tpu as pltpu
from jax.sharding import PartitionSpec as P

F32 = jnp.float32
BF16 = jnp.bfloat16
TRANS_B = (((1,), (1,)), ((), ()))


def params(mib=48):
    return pltpu.CompilerParams(vmem_limit_bytes=mib * 1024 * 1024)


def route_kernel(capacity, ids_ref, w_ref, tok_ref, og_ref, dy_ref, x_ref, pt_ref, scaled_ref):
    top, tok = ids_ref.shape
    rows = top * tok
    slots = dy_ref.shape[0]
    c_row = lax.broadcasted_iota(jnp.int32, (rows, tok), 0)
    pick_i = (c_row % tok == lax.broadcasted_iota(jnp.int32, (rows, tok), 1)).astype(BF16)
    c_k = lax.broadcasted_iota(jnp.int32, (rows, top), 0)
    pick_k = (c_k // tok == lax.broadcasted_iota(jnp.int32, (rows, top), 1)).astype(F32)

    def column(values):
        spread = lax.dot_general(pick_i, values, TRANS_B, preferred_element_type=F32)
        return jnp.sum(spread * pick_k, axis=1, keepdims=True)

    ids_col = column(ids_ref[...].astype(F32).astype(BF16))
    w = w_ref[...]
    w_hi = w.astype(BF16)
    rest = w - w_hi.astype(F32)
    w_mid = rest.astype(BF16)
    w_lo = (rest - w_mid.astype(F32)).astype(BF16)
    w_col = column(w_hi) + (column(w_mid) + column(w_lo))
    sub = lax.broadcasted_iota(jnp.int32, (rows, rows), 0)
    lane = lax.broadcasted_iota(jnp.int32, (rows, rows), 1)
    ids_row = jnp.sum(jnp.where(sub == lane, ids_col, 0.0), axis=0, keepdims=True)
    order_sub = (sub % tok) * top + sub // tok
    order_lane = (lane % tok) * top + lane // tok
    earlier = (ids_col == ids_row) & (order_sub < order_lane)
    slot_row = jnp.sum(jnp.where(earlier, 1.0, 0.0), axis=0, keepdims=True)
    code = jnp.where(slot_row < capacity, ids_row * capacity + slot_row, -1.0).astype(jnp.int32)
    table = (lax.broadcasted_iota(jnp.int32, (slots, rows), 0) == code).astype(F32).astype(BF16)
    per_token = jnp.dot(table, pick_i, preferred_element_type=F32).astype(BF16)
    pt_ref[...] = lax.dot_general(
        pick_i, table, (((0,), (1,)), ((), ())), preferred_element_type=F32
    ).astype(BF16)
    og = jnp.dot(pick_i, og_ref[...], preferred_element_type=F32)
    scaled_ref[...] = (w_col * og).astype(BF16)
    dy_ref[...] = jnp.dot(table, scaled_ref[...], preferred_element_type=F32).astype(BF16)
    x_ref[...] = jnp.dot(per_token, tok_ref[...], preferred_element_type=F32).astype(BF16)


def route(tokens, out_grad, expert_ids, route_weights, experts, capacity):
    tok, width = tokens.shape
    top = expert_ids.shape[1]
    slots = experts * capacity
    return pl.pallas_call(
        lambda *refs: route_kernel(capacity, *refs),
        out_shape=(
            jax.ShapeDtypeStruct((slots, width), BF16),
            jax.ShapeDtypeStruct((slots, width), BF16),
            jax.ShapeDtypeStruct((tok, slots), BF16),
        ),
        scratch_shapes=[pltpu.VMEM((tok * top, width), BF16)],
        compiler_params=params(),
        name="route",
    )(expert_ids.T, route_weights.T, tokens, out_grad)


def hidden_kernel(dy_ref, w_ref, out_ref):
    part = out_ref.shape[2]
    out = lax.dot_general(dy_ref[...], w_ref[0], TRANS_B, preferred_element_type=F32)
    for j in range(out_ref.shape[0]):
        out_ref[j] = out[:, j * part : (j + 1) * part].astype(BF16)


def hidden_parts(dy_rows, w_down, n_rep):
    rows, width = dy_rows.shape
    part = w_down.shape[1] // n_rep
    per = 2
    return pl.pallas_call(
        hidden_kernel,
        grid=(n_rep // per,),
        in_specs=[
            pl.BlockSpec((rows, width), lambda c: (0, 0)),
            pl.BlockSpec((1, per * part, width), lambda c: (0, c, 0)),
        ],
        out_specs=pl.BlockSpec((per, rows, part), lambda c: (c, 0, 0)),
        out_shape=jax.ShapeDtypeStruct((n_rep, rows, part), BF16),
        compiler_params=params(),
        name="hidden",
    )(dy_rows, w_down)


def gate_up_kernel(x_ref, wg_ref, wu_ref, out_ref):
    part = out_ref.shape[2]
    rows = x_ref.shape[0]
    gate = jnp.dot(x_ref[...], wg_ref[0], preferred_element_type=F32)
    up = jnp.dot(x_ref[...], wu_ref[0], preferred_element_type=F32)
    for j in range(out_ref.shape[0]):
        out_ref[j, :rows] = gate[:, j * part : (j + 1) * part].astype(BF16)
        out_ref[j, rows:] = up[:, j * part : (j + 1) * part].astype(BF16)


def gate_up_parts(x_rows, w_gate, w_up, n_rep):
    rows, width = x_rows.shape
    part = w_gate.shape[2] // n_rep
    per = 2
    w_spec = pl.BlockSpec((1, width, per * part), lambda c: (0, 0, c))
    return pl.pallas_call(
        gate_up_kernel,
        grid=(n_rep // per,),
        in_specs=[pl.BlockSpec((rows, width), lambda c: (0, 0)), w_spec, w_spec],
        out_specs=pl.BlockSpec((per, 2 * rows, part), lambda c: (c, 0, 0)),
        out_shape=jax.ShapeDtypeStruct((n_rep, 2 * rows, part), BF16),
        compiler_params=params(),
        name="gate_up",
    )(x_rows, w_gate, w_up)


def activate_kernel(h_ref, g_ref, u_ref, out_ref):
    part = h_ref.shape[2]
    hidden = jnp.sum(h_ref[...].astype(F32), axis=0)
    gate = jnp.sum(g_ref[...].astype(F32), axis=0)
    up = jnp.sum(u_ref[...].astype(F32), axis=0)
    s = jax.nn.sigmoid(gate)
    out_ref[:, :part] = (hidden * up * s * (1.0 + gate * (1.0 - s))).astype(BF16)
    out_ref[:, part:] = (hidden * gate * s).astype(BF16)


def activate(hid, gu):
    n_rep, rows, part = hid.shape
    block = 128
    blocks = rows // block
    return pl.pallas_call(
        activate_kernel,
        grid=(blocks,),
        in_specs=[
            pl.BlockSpec((n_rep, block, part), lambda i: (0, i, 0)),
            pl.BlockSpec((n_rep, block, part), lambda i: (0, i, 0)),
            pl.BlockSpec((n_rep, block, part), lambda i: (0, blocks + i, 0)),
        ],
        out_specs=pl.BlockSpec((block, 2 * part), lambda i: (i, 0)),
        out_shape=jax.ShapeDtypeStruct((rows, 2 * part), BF16),
        compiler_params=params(),
        name="activate",
    )(hid, gu, gu)


def row_grad_kernel(r_ref, wg_ref, wu_ref, out_ref, acc_ref):
    c = pl.program_id(0)
    part = r_ref.shape[2] // 2
    total = None
    for j in range(r_ref.shape[0]):
        cols = slice(j * part, (j + 1) * part)
        term = lax.dot_general(
            r_ref[j, :, :part], wg_ref[0, :, cols], TRANS_B, preferred_element_type=F32
        ) + lax.dot_general(
            r_ref[j, :, part:], wu_ref[0, :, cols], TRANS_B, preferred_element_type=F32
        )
        total = term if total is None else total + term

    @pl.when(c == 0)
    def _():
        acc_ref[...] = total

    @pl.when(c > 0)
    def _():
        acc_ref[...] += total

    @pl.when(c == pl.num_programs(0) - 1)
    def _():
        out_ref[...] = acc_ref[...].astype(BF16)


def row_grad(rows_all, w_gate, w_up):
    n_rep, rows, part2 = rows_all.shape
    part = part2 // 2
    width = w_gate.shape[1]
    per = 2
    w_spec = pl.BlockSpec((1, width, per * part), lambda c: (0, 0, c))
    return pl.pallas_call(
        row_grad_kernel,
        grid=(n_rep // per,),
        in_specs=[pl.BlockSpec((per, rows, part2), lambda c: (c, 0, 0)), w_spec, w_spec],
        out_specs=pl.BlockSpec((rows, width), lambda c: (0, 0)),
        out_shape=jax.ShapeDtypeStruct((rows, width), BF16),
        scratch_shapes=[pltpu.VMEM((rows, width), F32)],
        compiler_params=params(),
        name="row_grad",
    )(rows_all, w_gate, w_up)


def per_device(tokens, out_grad, expert_ids, route_weights, gate_weight, up_weight, down_weight):
    tok, width = tokens.shape
    top = expert_ids.shape[1]
    n_rep = lax.axis_size("rep")
    experts = lax.axis_size("outer") * lax.axis_size("local")
    capacity = max(2, 2 * tok * top // experts)
    slots = experts * capacity
    both = ("outer", "local")
    send_dy, send_x, per_token_t = route(
        tokens, out_grad, expert_ids, route_weights, experts, capacity
    )

    def exchange(rows):
        blocks = rows.reshape(experts, capacity, width)
        return lax.all_to_all(blocks, both, 0, 0, tiled=True).reshape(slots, width)

    def over_rep(parts):
        return lax.all_to_all(parts, "rep", 0, 0, tiled=True)

    dy_rows = exchange(send_dy)
    x_rows = exchange(send_x)
    hid = over_rep(hidden_parts(dy_rows, down_weight, n_rep))
    gu = over_rep(gate_up_parts(x_rows, gate_weight, up_weight, n_rep))
    own = activate(hid, gu)
    rows_all = over_rep(jnp.broadcast_to(own[None], (n_rep,) + own.shape))
    returned = exchange(row_grad(rows_all, gate_weight, up_weight))
    return jnp.dot(per_token_t, returned, preferred_element_type=F32).astype(BF16)


def solution(mesh):
    return jax.shard_map(
        per_device,
        mesh=mesh,
        in_specs=(
            P(("outer", "local"), "rep"),
            P(("outer", "local"), "rep"),
            P(("outer", "local"), None),
            P(("outer", "local"), None),
            P(("outer", "local"), "rep", None),
            P(("outer", "local"), "rep", None),
            P(("outer", "local"), None, "rep"),
        ),
        out_specs=P(("outer", "local"), "rep"),
        check_vma=False,
    )
```

```python
import jax
import jax.numpy as jnp
from jax import lax
from jax.experimental import pallas as pl
from jax.experimental.pallas import tpu as pltpu
from jax.sharding import PartitionSpec as P

F32 = jnp.float32
BF16 = jnp.bfloat16
TRANS_B = (((1,), (1,)), ((), ()))


def params(mib=48):
    return pltpu.CompilerParams(vmem_limit_bytes=mib * 1024 * 1024)


def route_kernel(capacity, ids_ref, w_ref, tok_ref, og_ref, dy_ref, x_ref, pt_ref, scaled_ref):
    top, tok = ids_ref.shape
    rows = top * tok
    slots = dy_ref.shape[0]
    c_row = lax.broadcasted_iota(jnp.int32, (rows, tok), 0)
    pick_i = (c_row % tok == lax.broadcasted_iota(jnp.int32, (rows, tok), 1)).astype(BF16)
    c_k = lax.broadcasted_iota(jnp.int32, (rows, top), 0)
    pick_k = (c_k // tok == lax.broadcasted_iota(jnp.int32, (rows, top), 1)).astype(F32)

    def column(values):
        spread = lax.dot_general(pick_i, values, TRANS_B, preferred_element_type=F32)
        return jnp.sum(spread * pick_k, axis=1, keepdims=True)

    ids_col = column(ids_ref[...].astype(F32).astype(BF16))
    w = w_ref[...]
    w_hi = w.astype(BF16)
    rest = w - w_hi.astype(F32)
    w_mid = rest.astype(BF16)
    w_lo = (rest - w_mid.astype(F32)).astype(BF16)
    w_col = column(w_hi) + (column(w_mid) + column(w_lo))
    sub = lax.broadcasted_iota(jnp.int32, (rows, rows), 0)
    lane = lax.broadcasted_iota(jnp.int32, (rows, rows), 1)
    ids_row = jnp.sum(jnp.where(sub == lane, ids_col, 0.0), axis=0, keepdims=True)
    order_sub = (sub % tok) * top + sub // tok
    order_lane = (lane % tok) * top + lane // tok
    earlier = (ids_col == ids_row) & (order_sub < order_lane)
    slot_row = jnp.sum(jnp.where(earlier, 1.0, 0.0), axis=0, keepdims=True)
    code = jnp.where(slot_row < capacity, ids_row * capacity + slot_row, -1.0).astype(jnp.int32)
    table = (lax.broadcasted_iota(jnp.int32, (slots, rows), 0) == code).astype(F32).astype(BF16)
    per_token = jnp.dot(table, pick_i, preferred_element_type=F32).astype(BF16)
    pt_ref[...] = lax.dot_general(
        pick_i, table, (((0,), (1,)), ((), ())), preferred_element_type=F32
    ).astype(BF16)
    og = jnp.dot(pick_i, og_ref[...], preferred_element_type=F32)
    scaled_ref[...] = (w_col * og).astype(BF16)
    dy_ref[...] = jnp.dot(table, scaled_ref[...], preferred_element_type=F32).astype(BF16)
    x_ref[...] = jnp.dot(per_token, tok_ref[...], preferred_element_type=F32).astype(BF16)


def route(tokens, out_grad, expert_ids, route_weights, experts, capacity):
    tok, width = tokens.shape
    top = expert_ids.shape[1]
    slots = experts * capacity
    return pl.pallas_call(
        lambda *refs: route_kernel(capacity, *refs),
        out_shape=(
            jax.ShapeDtypeStruct((slots, width), BF16),
            jax.ShapeDtypeStruct((slots, width), BF16),
            jax.ShapeDtypeStruct((tok, slots), BF16),
        ),
        scratch_shapes=[pltpu.VMEM((tok * top, width), BF16)],
        compiler_params=params(),
        name="route",
    )(expert_ids.T, route_weights.T, tokens, out_grad)


def hidden_kernel(dy_ref, w_ref, out_ref):
    part = out_ref.shape[2]
    out = lax.dot_general(dy_ref[...], w_ref[0], TRANS_B, preferred_element_type=F32)
    for j in range(out_ref.shape[0]):
        out_ref[j] = out[:, j * part : (j + 1) * part].astype(BF16)


def hidden_parts(dy_rows, w_down, n_rep):
    rows, width = dy_rows.shape
    part = w_down.shape[1] // n_rep
    per = 2
    return pl.pallas_call(
        hidden_kernel,
        grid=(n_rep // per,),
        in_specs=[
            pl.BlockSpec((rows, width), lambda c: (0, 0)),
            pl.BlockSpec((1, per * part, width), lambda c: (0, c, 0)),
        ],
        out_specs=pl.BlockSpec((per, rows, part), lambda c: (c, 0, 0)),
        out_shape=jax.ShapeDtypeStruct((n_rep, rows, part), BF16),
        compiler_params=params(),
        name="hidden",
    )(dy_rows, w_down)


def gate_up_kernel(x_ref, wg_ref, wu_ref, out_ref):
    part = wg_ref.shape[2]
    out_ref[0, :, :part] = jnp.dot(x_ref[...], wg_ref[0], preferred_element_type=F32)
    out_ref[0, :, part:] = jnp.dot(x_ref[...], wu_ref[0], preferred_element_type=F32)


def gate_up_parts(x_rows, w_gate, w_up, n_rep):
    rows, width = x_rows.shape
    part = w_gate.shape[2] // n_rep
    w_spec = pl.BlockSpec((1, width, part), lambda c: (0, 0, c))
    return pl.pallas_call(
        gate_up_kernel,
        grid=(n_rep,),
        in_specs=[pl.BlockSpec((rows, width), lambda c: (0, 0)), w_spec, w_spec],
        out_specs=pl.BlockSpec((1, rows, 2 * part), lambda c: (c, 0, 0)),
        out_shape=jax.ShapeDtypeStruct((n_rep, rows, 2 * part), F32),
        compiler_params=params(),
        name="gate_up",
    )(x_rows, w_gate, w_up)


def activate_kernel(h_ref, gu_ref, out_ref):
    part = h_ref.shape[2]
    hidden = jnp.sum(h_ref[...].astype(F32), axis=0)
    gate = gu_ref[:, :part]
    up = gu_ref[:, part:]
    s = jax.nn.sigmoid(gate)
    out_ref[:, :part] = (hidden * up * s * (1.0 + gate * (1.0 - s))).astype(BF16)
    out_ref[:, part:] = (hidden * gate * s).astype(BF16)


def activate(hid, gate_up):
    n_rep, rows, part = hid.shape
    block = 128
    return pl.pallas_call(
        activate_kernel,
        grid=(rows // block,),
        in_specs=[
            pl.BlockSpec((n_rep, block, part), lambda i: (0, i, 0)),
            pl.BlockSpec((block, 2 * part), lambda i: (i, 0)),
        ],
        out_specs=pl.BlockSpec((block, 2 * part), lambda i: (i, 0)),
        out_shape=jax.ShapeDtypeStruct((rows, 2 * part), BF16),
        compiler_params=params(),
        name="activate",
    )(hid, gate_up)


def row_grad_kernel(offsets, has_start, n_rep, me_ref, *refs):
    blocks = refs[: len(offsets)]
    wg_ref, wu_ref = refs[len(offsets) : len(offsets) + 2]
    out_ref = refs[-1]
    part = blocks[0].shape[1] // 2
    total = refs[-2][...] if has_start else None
    for offset, block in zip(offsets, blocks):
        c = lax.rem(me_ref[0] + offset, n_rep)
        cols = pl.ds(pl.multiple_of(c * part, part), part)
        weights = jnp.concatenate([wg_ref[0, :, cols], wu_ref[0, :, cols]], axis=1)
        term = lax.dot_general(block[...], weights, TRANS_B, preferred_element_type=F32)
        total = term if total is None else total + term
    out_ref[...] = total.astype(out_ref.dtype)


def row_grad(me, blocks, offsets, w_gate, w_up, n_rep, start, dtype, name):
    rows = blocks[0].shape[0]
    width = w_gate.shape[1]
    vmem = pl.BlockSpec(memory_space=pltpu.VMEM)
    extra = () if start is None else (start,)
    return pl.pallas_call(
        lambda *refs: row_grad_kernel(offsets, start is not None, n_rep, *refs),
        in_specs=[pl.BlockSpec(memory_space=pltpu.SMEM)]
        + [vmem] * (len(blocks) + 2 + len(extra)),
        out_specs=vmem,
        out_shape=jax.ShapeDtypeStruct((rows, width), dtype),
        compiler_params=params(),
        name=name,
    )(me, *blocks, w_gate, w_up, *extra)


def gather_matmul(own, w_gate, w_up, n_rep):
    me = lax.axis_index("rep").astype(jnp.int32).reshape(1)

    def shift(rows, by):
        return lax.ppermute(rows, "rep", [(i, (i + by) % n_rep) for i in range(n_rep)])

    blocks, offsets = [own], [0]
    up = down = own
    for step in range(1, n_rep // 2):
        up, down = shift(up, 1), shift(down, -1)
        blocks += [up, down]
        offsets += [n_rep - step, step]
    half = own.shape[0] // 2
    far = jnp.concatenate([shift(up[:half], 1), shift(down[half:], -1)])
    early = len(blocks) - 2
    total = row_grad(
        me, blocks[:early], offsets[:early], w_gate, w_up, n_rep, None, F32, "row_grad_a"
    )
    return row_grad(
        me,
        blocks[early:] + [far],
        offsets[early:] + [n_rep // 2],
        w_gate,
        w_up,
        n_rep,
        total,
        BF16,
        "row_grad_b",
    )


def per_device(tokens, out_grad, expert_ids, route_weights, gate_weight, up_weight, down_weight):
    tok, width = tokens.shape
    top = expert_ids.shape[1]
    n_rep = lax.axis_size("rep")
    experts = lax.axis_size("outer") * lax.axis_size("local")
    capacity = max(2, 2 * tok * top // experts)
    slots = experts * capacity
    both = ("outer", "local")
    send_dy, send_x, per_token_t = route(
        tokens, out_grad, expert_ids, route_weights, experts, capacity
    )

    def exchange(rows):
        blocks = rows.reshape(experts, capacity, width)
        return lax.all_to_all(blocks, both, 0, 0, tiled=True).reshape(slots, width)

    def over_rep(parts):
        return lax.all_to_all(parts, "rep", 0, 0, tiled=True)

    x_rows = exchange(send_x)
    gate_up = lax.psum_scatter(
        gate_up_parts(x_rows, gate_weight, up_weight, n_rep), "rep", scatter_dimension=0
    )
    dy_rows = exchange(send_dy)
    hid = over_rep(hidden_parts(dy_rows, down_weight, n_rep))
    own = activate(hid, gate_up)
    returned = exchange(gather_matmul(own, gate_weight, up_weight, n_rep))
    return jnp.dot(per_token_t, returned, preferred_element_type=F32).astype(BF16)


def solution(mesh):
    return jax.shard_map(
        per_device,
        mesh=mesh,
        in_specs=(
            P(("outer", "local"), "rep"),
            P(("outer", "local"), "rep"),
            P(("outer", "local"), None),
            P(("outer", "local"), None),
            P(("outer", "local"), "rep", None),
            P(("outer", "local"), "rep", None),
            P(("outer", "local"), None, "rep"),
        ),
        out_specs=P(("outer", "local"), "rep"),
        check_vma=False,
    )
```

```python
import jax
import jax.numpy as jnp
from jax import lax
from jax.experimental import pallas as pl
from jax.experimental.pallas import tpu as pltpu
from jax.sharding import PartitionSpec as P

F32 = jnp.float32
BF16 = jnp.bfloat16
TRANS_B = (((1,), (1,)), ((), ()))
VMEM_SPEC = pl.BlockSpec(memory_space=pltpu.VMEM)


def params(mib=16):
    return pltpu.CompilerParams(vmem_limit_bytes=mib * 1024 * 1024)


def route_kernel(capacity, ids_hbm, w_hbm, tok_hbm, og_hbm, send_ref, pt_ref, *scratch):
    ids_ref, w_ref, tok_ref, og_ref, scaled_ref, sems = scratch
    copies = [
        pltpu.make_async_copy(src, dst, sems.at[n])
        for n, (src, dst) in enumerate(
            ((ids_hbm, ids_ref), (w_hbm, w_ref), (og_hbm, og_ref), (tok_hbm, tok_ref))
        )
    ]
    for copy in copies:
        copy.start()
    top, tok = ids_ref.shape
    width = tok_ref.shape[1]
    rows = top * tok
    slots = send_ref.shape[0]
    c_row = lax.broadcasted_iota(jnp.int32, (rows, tok), 0)
    pick_i = (c_row % tok == lax.broadcasted_iota(jnp.int32, (rows, tok), 1)).astype(BF16)
    c_k = lax.broadcasted_iota(jnp.int32, (rows, top), 0)
    pick_k = (c_k // tok == lax.broadcasted_iota(jnp.int32, (rows, top), 1)).astype(F32)
    sub = lax.broadcasted_iota(jnp.int32, (rows, rows), 0)
    lane = lax.broadcasted_iota(jnp.int32, (rows, rows), 1)
    order_sub = (sub % tok) * top + sub // tok
    order_lane = (lane % tok) * top + lane // tok
    for copy in copies:
        copy.wait()

    def column(values):
        spread = lax.dot_general(pick_i, values, TRANS_B, preferred_element_type=F32)
        return jnp.sum(spread * pick_k, axis=1, keepdims=True)

    ids_col = column(ids_ref[...].astype(F32).astype(BF16))
    w = w_ref[...]
    w_hi = w.astype(BF16)
    rest = w - w_hi.astype(F32)
    w_mid = rest.astype(BF16)
    w_lo = (rest - w_mid.astype(F32)).astype(BF16)
    w_col = column(w_hi) + (column(w_mid) + column(w_lo))
    ids_row = jnp.sum(jnp.where(sub == lane, ids_col, 0.0), axis=0, keepdims=True)
    earlier = (ids_col == ids_row) & (order_sub < order_lane)
    slot_row = jnp.sum(jnp.where(earlier, 1.0, 0.0), axis=0, keepdims=True)
    code = jnp.where(slot_row < capacity, ids_row * capacity + slot_row, -1.0).astype(jnp.int32)
    table = (lax.broadcasted_iota(jnp.int32, (slots, rows), 0) == code).astype(F32).astype(BF16)
    per_token = jnp.dot(table, pick_i, preferred_element_type=F32).astype(BF16)
    pt_ref[...] = lax.dot_general(
        pick_i, table, (((0,), (1,)), ((), ())), preferred_element_type=F32
    ).astype(BF16)
    og = jnp.dot(pick_i, og_ref[...], preferred_element_type=F32)
    scaled_ref[...] = (w_col * og).astype(BF16)
    send_ref[:, :width] = jnp.dot(
        per_token, tok_ref[...], preferred_element_type=F32
    ).astype(BF16)
    send_ref[:, width:] = jnp.dot(
        table, scaled_ref[...], preferred_element_type=F32
    ).astype(BF16)


def route(tokens, out_grad, expert_ids, route_weights, experts, capacity):
    tok, width = tokens.shape
    top = expert_ids.shape[1]
    slots = experts * capacity
    return pl.pallas_call(
        lambda *refs: route_kernel(capacity, *refs),
        in_specs=[pl.BlockSpec(memory_space=pltpu.HBM)] * 4,
        out_specs=(VMEM_SPEC, VMEM_SPEC),
        out_shape=(
            jax.ShapeDtypeStruct((slots, 2 * width), BF16),
            jax.ShapeDtypeStruct((tok, slots), BF16),
        ),
        scratch_shapes=[
            pltpu.VMEM((top, tok), jnp.int32),
            pltpu.VMEM((top, tok), F32),
            pltpu.VMEM((tok, width), BF16),
            pltpu.VMEM((tok, width), BF16),
            pltpu.VMEM((tok * top, width), BF16),
            pltpu.SemaphoreType.DMA((4,)),
        ],
        compiler_params=params(63),
        name="route",
    )(expert_ids.T, route_weights.T, tokens, out_grad)


def hidden_kernel(rows_ref, w_ref, out_ref):
    part = out_ref.shape[2]
    out = lax.dot_general(rows_ref[...], w_ref[0], TRANS_B, preferred_element_type=F32)
    for j in range(out_ref.shape[0]):
        out_ref[j] = out[:, j * part : (j + 1) * part]


def hidden_parts(both_rows, w_down, n_rep):
    rows = both_rows.shape[0]
    width = both_rows.shape[1] // 2
    part = w_down.shape[1] // n_rep
    per = 2
    return pl.pallas_call(
        hidden_kernel,
        grid=(n_rep // per,),
        in_specs=[
            pl.BlockSpec((rows, width), lambda c: (0, 1)),
            pl.BlockSpec((1, per * part, width), lambda c: (0, c, 0)),
        ],
        out_specs=pl.BlockSpec((per, rows, part), lambda c: (c, 0, 0)),
        out_shape=jax.ShapeDtypeStruct((n_rep, rows, part), F32),
        compiler_params=params(62),
        name="hidden",
    )(both_rows, w_down)


def chunk_weights(me_ref, offset, n_rep, wg_ref, wu_ref):
    part = wg_ref.shape[2] // n_rep
    c = lax.rem(me_ref[0] + offset, n_rep)
    cols = pl.ds(pl.multiple_of(c * part, part), part)
    return jnp.concatenate([wg_ref[0, :, cols], wu_ref[0, :, cols]], axis=1)


def gate_up_kernel(offset, n_rep, me_ref, rows_ref, wg_ref, wu_ref, *refs):
    width = wg_ref.shape[1]
    weights = chunk_weights(me_ref, offset, n_rep, wg_ref, wu_ref)
    total = jnp.dot(rows_ref[:, :width], weights, preferred_element_type=F32)
    for arrived in refs[:-1]:
        total = total + arrived[...].astype(F32)
    refs[-1][...] = total.astype(refs[-1].dtype)


def gate_up(me, both_rows, w_gate, w_up, n_rep, offset, arrived, dtype, name):
    rows = both_rows.shape[0]
    part = w_gate.shape[2] // n_rep
    return pl.pallas_call(
        lambda *refs: gate_up_kernel(offset, n_rep, *refs),
        in_specs=[pl.BlockSpec(memory_space=pltpu.SMEM)] + [VMEM_SPEC] * (3 + len(arrived)),
        out_specs=VMEM_SPEC,
        out_shape=jax.ShapeDtypeStruct((rows, 2 * part), dtype),
        compiler_params=params(),
        name=name,
    )(me, both_rows, w_gate, w_up, *arrived)


def shift(rows, by):
    n_rep = lax.axis_size("rep")
    return lax.ppermute(rows, "rep", [(i, (i + by) % n_rep) for i in range(n_rep)])


def gate_up_sums(me, both_rows, w_gate, w_up, n_rep):
    half = n_rep // 2
    up, down = (), ()
    for hop in range(half, 0, -1):
        term = gate_up(
            me, both_rows, w_gate, w_up, n_rep, hop, up, BF16, "gate_up_rise_%d" % hop
        )
        up = (shift(term, 1),)
        if hop < half:
            term = gate_up(
                me, both_rows, w_gate, w_up, n_rep, n_rep - hop, down, BF16, "gate_up_fall_%d" % hop
            )
            down = (shift(term, -1),)
    own = gate_up(me, both_rows, w_gate, w_up, n_rep, 0, (), F32, "gate_up_own")
    return own, up[0], down[0]


def activate_kernel(h_ref, own_ref, up_ref, down_ref, out_ref):
    part = h_ref.shape[1]
    sums = own_ref[...] + up_ref[...].astype(F32) + down_ref[...].astype(F32)
    hidden = h_ref[...]
    gate = sums[:, :part]
    up = sums[:, part:]
    s = jax.nn.sigmoid(gate)
    out_ref[:, :part] = (hidden * up * s * (1.0 + gate * (1.0 - s))).astype(BF16)
    out_ref[:, part:] = (hidden * gate * s).astype(BF16)


def activate(hidden, own, up, down):
    rows, part2 = own.shape
    block = 128
    spec = pl.BlockSpec((block, part2), lambda i: (i, 0))
    return pl.pallas_call(
        activate_kernel,
        grid=(rows // block,),
        in_specs=[pl.BlockSpec((block, part2 // 2), lambda i: (i, 0)), spec, spec, spec],
        out_specs=spec,
        out_shape=jax.ShapeDtypeStruct(own.shape, BF16),
        compiler_params=params(62),
        name="activate",
    )(hidden, own, up, down)


def row_grad_kernel(offsets, has_start, n_rep, me_ref, *refs):
    blocks = refs[: len(offsets)]
    wg_ref, wu_ref = refs[len(offsets) : len(offsets) + 2]
    out_ref = refs[-1]
    total = refs[-2][...] if has_start else None
    for offset, block in zip(offsets, blocks):
        weights = chunk_weights(me_ref, offset, n_rep, wg_ref, wu_ref)
        term = lax.dot_general(block[...], weights, TRANS_B, preferred_element_type=F32)
        total = term if total is None else total + term
    out_ref[...] = total.astype(out_ref.dtype)


def row_grad(me, blocks, offsets, w_gate, w_up, n_rep, start, dtype, name):
    rows = blocks[0].shape[0]
    width = w_gate.shape[1]
    extra = () if start is None else (start,)
    return pl.pallas_call(
        lambda *refs: row_grad_kernel(offsets, start is not None, n_rep, *refs),
        in_specs=[pl.BlockSpec(memory_space=pltpu.SMEM)]
        + [VMEM_SPEC] * (len(blocks) + 2 + len(extra)),
        out_specs=VMEM_SPEC,
        out_shape=jax.ShapeDtypeStruct((rows, width), dtype),
        compiler_params=params(),
        name=name,
    )(me, *blocks, w_gate, w_up, *extra)


def gather_matmul(me, own, w_gate, w_up, n_rep):
    half = n_rep // 2
    blocks, offsets = [own], [0]
    up = down = own
    for step in range(1, half):
        up, down = shift(up, 1), shift(down, -1)
        blocks += [up, down]
        offsets += [n_rep - step, step]
    last = shift(up, 1)
    total = row_grad(me, blocks, offsets, w_gate, w_up, n_rep, None, F32, "row_grad_near")
    return row_grad(me, [last], [half], w_gate, w_up, n_rep, total, BF16, "row_grad_far")


def per_device(tokens, out_grad, expert_ids, route_weights, gate_weight, up_weight, down_weight):
    tok, width = tokens.shape
    top = expert_ids.shape[1]
    n_rep = lax.axis_size("rep")
    experts = lax.axis_size("outer") * lax.axis_size("local")
    capacity = max(2, 2 * tok * top // experts)
    slots = experts * capacity
    me = lax.axis_index("rep").astype(jnp.int32).reshape(1)
    send, per_token_t = route(tokens, out_grad, expert_ids, route_weights, experts, capacity)

    def exchange(rows):
        blocks = rows.reshape(experts, capacity, rows.shape[1])
        return lax.all_to_all(blocks, ("outer", "local"), 0, 0, tiled=True).reshape(rows.shape)

    both_rows = exchange(send)
    hidden = lax.psum_scatter(
        hidden_parts(both_rows, down_weight, n_rep), "rep", scatter_dimension=0
    )
    sums = gate_up_sums(me, both_rows, gate_weight, up_weight, n_rep)
    own = activate(hidden, *sums)
    returned = exchange(gather_matmul(me, own, gate_weight, up_weight, n_rep))
    return jnp.dot(per_token_t, returned, preferred_element_type=F32).astype(BF16)


def solution(mesh):
    return jax.shard_map(
        per_device,
        mesh=mesh,
        in_specs=(
            P(("outer", "local"), "rep"),
            P(("outer", "local"), "rep"),
            P(("outer", "local"), None),
            P(("outer", "local"), None),
            P(("outer", "local"), "rep", None),
            P(("outer", "local"), "rep", None),
            P(("outer", "local"), None, "rep"),
        ),
        out_specs=P(("outer", "local"), "rep"),
        check_vma=False,
    )
```

```python
import jax
import jax.numpy as jnp
from jax import lax
from jax.experimental import pallas as pl
from jax.experimental.pallas import tpu as pltpu
from jax.sharding import PartitionSpec as P

F32 = jnp.float32
BF16 = jnp.bfloat16
TRANS_B = (((1,), (1,)), ((), ()))
VMEM_SPEC = pl.BlockSpec(memory_space=pltpu.VMEM)


def params(mib=16):
    return pltpu.CompilerParams(vmem_limit_bytes=mib * 1024 * 1024)


def route_kernel(capacity, ids_hbm, w_hbm, tok_hbm, og_hbm, dy_ref, x_ref, pt_ref, *scratch):
    ids_ref, w_ref, tok_ref, og_ref, scaled_ref, sems = scratch
    copies = [
        pltpu.make_async_copy(src, dst, sems.at[n])
        for n, (src, dst) in enumerate(
            ((ids_hbm, ids_ref), (w_hbm, w_ref), (og_hbm, og_ref), (tok_hbm, tok_ref))
        )
    ]
    for copy in copies:
        copy.start()
    top, tok = ids_ref.shape
    rows = top * tok
    slots = dy_ref.shape[0]
    c_row = lax.broadcasted_iota(jnp.int32, (rows, tok), 0)
    pick_i = (c_row % tok == lax.broadcasted_iota(jnp.int32, (rows, tok), 1)).astype(BF16)
    c_k = lax.broadcasted_iota(jnp.int32, (rows, top), 0)
    pick_k = (c_k // tok == lax.broadcasted_iota(jnp.int32, (rows, top), 1)).astype(F32)
    sub = lax.broadcasted_iota(jnp.int32, (rows, rows), 0)
    lane = lax.broadcasted_iota(jnp.int32, (rows, rows), 1)
    order_sub = (sub % tok) * top + sub // tok
    order_lane = (lane % tok) * top + lane // tok
    for copy in copies:
        copy.wait()

    def column(values):
        spread = lax.dot_general(pick_i, values, TRANS_B, preferred_element_type=F32)
        return jnp.sum(spread * pick_k, axis=1, keepdims=True)

    ids_col = column(ids_ref[...].astype(F32).astype(BF16))
    w = w_ref[...]
    w_hi = w.astype(BF16)
    rest = w - w_hi.astype(F32)
    w_mid = rest.astype(BF16)
    w_lo = (rest - w_mid.astype(F32)).astype(BF16)
    w_col = column(w_hi) + (column(w_mid) + column(w_lo))
    ids_row = jnp.sum(jnp.where(sub == lane, ids_col, 0.0), axis=0, keepdims=True)
    earlier = (ids_col == ids_row) & (order_sub < order_lane)
    slot_row = jnp.sum(jnp.where(earlier, 1.0, 0.0), axis=0, keepdims=True)
    code = jnp.where(slot_row < capacity, ids_row * capacity + slot_row, -1.0).astype(jnp.int32)
    table = (lax.broadcasted_iota(jnp.int32, (slots, rows), 0) == code).astype(F32).astype(BF16)
    per_token = jnp.dot(table, pick_i, preferred_element_type=F32).astype(BF16)
    pt_ref[...] = lax.dot_general(
        pick_i, table, (((0,), (1,)), ((), ())), preferred_element_type=F32
    ).astype(BF16)
    og = jnp.dot(pick_i, og_ref[...], preferred_element_type=F32)
    scaled_ref[...] = (w_col * og).astype(BF16)
    x_ref[...] = jnp.dot(per_token, tok_ref[...], preferred_element_type=F32).astype(BF16)
    dy_ref[...] = jnp.dot(table, scaled_ref[...], preferred_element_type=F32).astype(BF16)


def route(tokens, out_grad, expert_ids, route_weights, experts, capacity):
    tok, width = tokens.shape
    top = expert_ids.shape[1]
    slots = experts * capacity
    return pl.pallas_call(
        lambda *refs: route_kernel(capacity, *refs),
        in_specs=[pl.BlockSpec(memory_space=pltpu.HBM)] * 4,
        out_specs=(VMEM_SPEC, VMEM_SPEC, VMEM_SPEC),
        out_shape=(
            jax.ShapeDtypeStruct((slots, width), BF16),
            jax.ShapeDtypeStruct((slots, width), BF16),
            jax.ShapeDtypeStruct((tok, slots), BF16),
        ),
        scratch_shapes=[
            pltpu.VMEM((top, tok), jnp.int32),
            pltpu.VMEM((top, tok), F32),
            pltpu.VMEM((tok, width), BF16),
            pltpu.VMEM((tok, width), BF16),
            pltpu.VMEM((tok * top, width), BF16),
            pltpu.SemaphoreType.DMA((4,)),
        ],
        compiler_params=params(63),
        name="route",
    )(expert_ids.T, route_weights.T, tokens, out_grad)


def hidden_kernel(rows_ref, w_ref, out_ref):
    part = out_ref.shape[2]
    out = lax.dot_general(rows_ref[...], w_ref[0], TRANS_B, preferred_element_type=F32)
    for j in range(out_ref.shape[0]):
        out_ref[j] = out[:, j * part : (j + 1) * part]


def hidden_parts(dy_rows, w_down, n_rep):
    rows, width = dy_rows.shape
    part = w_down.shape[1] // n_rep
    per = 2
    return pl.pallas_call(
        hidden_kernel,
        grid=(n_rep // per,),
        in_specs=[
            pl.BlockSpec((rows, width), lambda c: (0, 0)),
            pl.BlockSpec((1, per * part, width), lambda c: (0, c, 0)),
        ],
        out_specs=pl.BlockSpec((per, rows, part), lambda c: (c, 0, 0)),
        out_shape=jax.ShapeDtypeStruct((n_rep, rows, part), F32),
        compiler_params=params(),
        name="hidden",
    )(dy_rows, w_down)


def chunk_weights(me_ref, offset, n_rep, wg_ref, wu_ref):
    part = wg_ref.shape[2] // n_rep
    c = lax.rem(me_ref[0] + offset, n_rep)
    cols = pl.ds(pl.multiple_of(c * part, part), part)
    return jnp.concatenate([wg_ref[0, :, cols], wu_ref[0, :, cols]], axis=1)


def gate_up_kernel(offset, n_rep, me_ref, rows_ref, wg_ref, wu_ref, *refs):
    weights = chunk_weights(me_ref, offset, n_rep, wg_ref, wu_ref)
    total = jnp.dot(rows_ref[...], weights, preferred_element_type=F32)
    for arrived in refs[:-1]:
        total = total + arrived[...].astype(F32)
    refs[-1][...] = total.astype(refs[-1].dtype)


def gate_up(me, x_rows, w_gate, w_up, n_rep, offset, arrived, dtype, name):
    rows = x_rows.shape[0]
    part = w_gate.shape[2] // n_rep
    return pl.pallas_call(
        lambda *refs: gate_up_kernel(offset, n_rep, *refs),
        in_specs=[pl.BlockSpec(memory_space=pltpu.SMEM)] + [VMEM_SPEC] * (3 + len(arrived)),
        out_specs=VMEM_SPEC,
        out_shape=jax.ShapeDtypeStruct((rows, 2 * part), dtype),
        compiler_params=params(),
        name=name,
    )(me, x_rows, w_gate, w_up, *arrived)


def shift(rows, by):
    n_rep = lax.axis_size("rep")
    return lax.ppermute(rows, "rep", [(i, (i + by) % n_rep) for i in range(n_rep)])


def gate_up_sums(me, x_rows, w_gate, w_up, n_rep):
    half = n_rep // 2
    up, down = (), ()
    for hop in range(half, 0, -1):
        term = gate_up(
            me, x_rows, w_gate, w_up, n_rep, hop, up, BF16, "gate_up_rise_%d" % hop
        )
        up = (shift(term, 1),)
        if hop < half:
            term = gate_up(
                me, x_rows, w_gate, w_up, n_rep, n_rep - hop, down, BF16, "gate_up_fall_%d" % hop
            )
            down = (shift(term, -1),)
    own = gate_up(me, x_rows, w_gate, w_up, n_rep, 0, (), F32, "gate_up_own")
    return own, up[0], down[0]


def activate_kernel(h_ref, own_ref, up_ref, down_ref, out_ref):
    part = h_ref.shape[1]
    sums = own_ref[...] + up_ref[...].astype(F32) + down_ref[...].astype(F32)
    hidden = h_ref[...]
    gate = sums[:, :part]
    up = sums[:, part:]
    s = jax.nn.sigmoid(gate)
    out_ref[:, :part] = (hidden * up * s * (1.0 + gate * (1.0 - s))).astype(BF16)
    out_ref[:, part:] = (hidden * gate * s).astype(BF16)


def activate(hidden, own, up, down):
    rows, part2 = own.shape
    block = 128
    spec = pl.BlockSpec((block, part2), lambda i: (i, 0))
    return pl.pallas_call(
        activate_kernel,
        grid=(rows // block,),
        in_specs=[pl.BlockSpec((block, part2 // 2), lambda i: (i, 0)), spec, spec, spec],
        out_specs=spec,
        out_shape=jax.ShapeDtypeStruct(own.shape, BF16),
        compiler_params=params(62),
        name="activate",
    )(hidden, own, up, down)


def row_grad_kernel(offsets, has_start, n_rep, me_ref, *refs):
    blocks = refs[: len(offsets)]
    wg_ref, wu_ref = refs[len(offsets) : len(offsets) + 2]
    out_ref = refs[-1]
    total = refs[-2][...] if has_start else None
    for offset, block in zip(offsets, blocks):
        weights = chunk_weights(me_ref, offset, n_rep, wg_ref, wu_ref)
        term = lax.dot_general(block[...], weights, TRANS_B, preferred_element_type=F32)
        total = term if total is None else total + term
    out_ref[...] = total.astype(out_ref.dtype)


def row_grad(me, blocks, offsets, w_gate, w_up, n_rep, start, dtype, name):
    rows = blocks[0].shape[0]
    width = w_gate.shape[1]
    extra = () if start is None else (start,)
    return pl.pallas_call(
        lambda *refs: row_grad_kernel(offsets, start is not None, n_rep, *refs),
        in_specs=[pl.BlockSpec(memory_space=pltpu.SMEM)]
        + [VMEM_SPEC] * (len(blocks) + 2 + len(extra)),
        out_specs=VMEM_SPEC,
        out_shape=jax.ShapeDtypeStruct((rows, width), dtype),
        compiler_params=params(),
        name=name,
    )(me, *blocks, w_gate, w_up, *extra)


def gather_matmul(me, own, w_gate, w_up, n_rep):
    half = n_rep // 2
    blocks, offsets = [own], [0]
    up = down = own
    for step in range(1, half):
        up, down = shift(up, 1), shift(down, -1)
        blocks += [up, down]
        offsets += [n_rep - step, step]
    last = shift(up, 1)
    total = row_grad(me, blocks, offsets, w_gate, w_up, n_rep, None, F32, "row_grad_near")
    return row_grad(me, [last], [half], w_gate, w_up, n_rep, total, BF16, "row_grad_far")


def per_device(tokens, out_grad, expert_ids, route_weights, gate_weight, up_weight, down_weight):
    tok, width = tokens.shape
    top = expert_ids.shape[1]
    n_rep = lax.axis_size("rep")
    experts = lax.axis_size("outer") * lax.axis_size("local")
    capacity = max(2, 2 * tok * top // experts)
    slots = experts * capacity
    me = lax.axis_index("rep").astype(jnp.int32).reshape(1)
    send_dy, send_x, per_token_t = route(
        tokens, out_grad, expert_ids, route_weights, experts, capacity
    )

    def exchange(rows):
        blocks = rows.reshape(experts, capacity, width)
        return lax.all_to_all(blocks, ("outer", "local"), 0, 0, tiled=True).reshape(slots, width)

    dy_rows = exchange(send_dy)
    hidden = lax.psum_scatter(
        hidden_parts(dy_rows, down_weight, n_rep), "rep", scatter_dimension=0
    )
    x_rows = exchange(send_x)
    sums = gate_up_sums(me, x_rows, gate_weight, up_weight, n_rep)
    own = activate(hidden, *sums)
    returned = exchange(gather_matmul(me, own, gate_weight, up_weight, n_rep))
    return jnp.dot(per_token_t, returned, preferred_element_type=F32).astype(BF16)


def solution(mesh):
    return jax.shard_map(
        per_device,
        mesh=mesh,
        in_specs=(
            P(("outer", "local"), "rep"),
            P(("outer", "local"), "rep"),
            P(("outer", "local"), None),
            P(("outer", "local"), None),
            P(("outer", "local"), "rep", None),
            P(("outer", "local"), "rep", None),
            P(("outer", "local"), None, "rep"),
        ),
        out_specs=P(("outer", "local"), "rep"),
        check_vma=False,
    )
```

```python
import jax
import jax.numpy as jnp
from jax import lax
from jax.experimental import pallas as pl
from jax.experimental.pallas import tpu as pltpu
from jax.sharding import PartitionSpec as P

F32 = jnp.float32
BF16 = jnp.bfloat16
TRANS_B = (((1,), (1,)), ((), ()))
VMEM_SPEC = pl.BlockSpec(memory_space=pltpu.VMEM)


def params(mib=16):
    return pltpu.CompilerParams(vmem_limit_bytes=mib * 1024 * 1024)


def route_kernel(capacity, ids_hbm, w_hbm, tok_hbm, og_hbm, dy_ref, x_ref, pt_ref, *scratch):
    ids_ref, w_ref, tok_ref, og_ref, scaled_ref, sems = scratch
    copies = [
        pltpu.make_async_copy(src, dst, sems.at[n])
        for n, (src, dst) in enumerate(
            ((ids_hbm, ids_ref), (w_hbm, w_ref), (og_hbm, og_ref), (tok_hbm, tok_ref))
        )
    ]
    for copy in copies:
        copy.start()
    top, tok = ids_ref.shape
    rows = top * tok
    slots = dy_ref.shape[0]
    c_row = lax.broadcasted_iota(jnp.int32, (rows, tok), 0)
    pick_i = (c_row % tok == lax.broadcasted_iota(jnp.int32, (rows, tok), 1)).astype(BF16)
    c_k = lax.broadcasted_iota(jnp.int32, (rows, top), 0)
    pick_k = (c_k // tok == lax.broadcasted_iota(jnp.int32, (rows, top), 1)).astype(F32)
    sub = lax.broadcasted_iota(jnp.int32, (rows, rows), 0)
    lane = lax.broadcasted_iota(jnp.int32, (rows, rows), 1)
    order_sub = (sub % tok) * top + sub // tok
    order_lane = (lane % tok) * top + lane // tok
    for copy in copies:
        copy.wait()

    def column(values):
        spread = lax.dot_general(pick_i, values, TRANS_B, preferred_element_type=F32)
        return jnp.sum(spread * pick_k, axis=1, keepdims=True)

    ids_col = column(ids_ref[...].astype(F32).astype(BF16))
    w = w_ref[...]
    w_hi = w.astype(BF16)
    rest = w - w_hi.astype(F32)
    w_mid = rest.astype(BF16)
    w_lo = (rest - w_mid.astype(F32)).astype(BF16)
    w_col = column(w_hi) + (column(w_mid) + column(w_lo))
    ids_row = jnp.sum(jnp.where(sub == lane, ids_col, 0.0), axis=0, keepdims=True)
    earlier = (ids_col == ids_row) & (order_sub < order_lane)
    slot_row = jnp.sum(jnp.where(earlier, 1.0, 0.0), axis=0, keepdims=True)
    code = jnp.where(slot_row < capacity, ids_row * capacity + slot_row, -1.0).astype(jnp.int32)
    table = (lax.broadcasted_iota(jnp.int32, (slots, rows), 0) == code).astype(F32).astype(BF16)
    per_token = jnp.dot(table, pick_i, preferred_element_type=F32).astype(BF16)
    pt_ref[...] = lax.dot_general(
        pick_i, table, (((0,), (1,)), ((), ())), preferred_element_type=F32
    ).astype(BF16)
    og = jnp.dot(pick_i, og_ref[...], preferred_element_type=F32)
    scaled_ref[...] = (w_col * og).astype(BF16)
    x_ref[...] = jnp.dot(per_token, tok_ref[...], preferred_element_type=F32).astype(BF16)
    dy_ref[...] = jnp.dot(table, scaled_ref[...], preferred_element_type=F32).astype(BF16)


def route(tokens, out_grad, expert_ids, route_weights, experts, capacity):
    tok, width = tokens.shape
    top = expert_ids.shape[1]
    slots = experts * capacity
    return pl.pallas_call(
        lambda *refs: route_kernel(capacity, *refs),
        in_specs=[pl.BlockSpec(memory_space=pltpu.HBM)] * 4,
        out_specs=(VMEM_SPEC, VMEM_SPEC, VMEM_SPEC),
        out_shape=(
            jax.ShapeDtypeStruct((slots, width), BF16),
            jax.ShapeDtypeStruct((slots, width), BF16),
            jax.ShapeDtypeStruct((tok, slots), BF16),
        ),
        scratch_shapes=[
            pltpu.VMEM((top, tok), jnp.int32),
            pltpu.VMEM((top, tok), F32),
            pltpu.VMEM((tok, width), BF16),
            pltpu.VMEM((tok, width), BF16),
            pltpu.VMEM((tok * top, width), BF16),
            pltpu.SemaphoreType.DMA((4,)),
        ],
        compiler_params=params(63),
        name="route",
    )(expert_ids.T, route_weights.T, tokens, out_grad)


def chunk_start(me_ref, offset, n_rep, part):
    return pl.multiple_of(lax.rem(me_ref[0] + offset, n_rep) * part, part)


def chunk_weights(me_ref, offset, n_rep, wg_ref, wu_ref):
    part = wg_ref.shape[2] // n_rep
    cols = pl.ds(chunk_start(me_ref, offset, n_rep, part), part)
    return jnp.concatenate([wg_ref[0, :, cols], wu_ref[0, :, cols]], axis=1)


def gate_up_kernel(x_ref, wg_ref, wu_ref, out_ref):
    per = out_ref.shape[0]
    part = wg_ref.shape[2] // per
    for j in range(per):
        cols = slice(j * part, (j + 1) * part)
        weights = jnp.concatenate([wg_ref[0, :, cols], wu_ref[0, :, cols]], axis=1)
        out_ref[j] = jnp.dot(x_ref[...], weights, preferred_element_type=F32)


def gate_up_parts(x_rows, w_gate, w_up, n_rep):
    rows, width = x_rows.shape
    part = w_gate.shape[2] // n_rep
    per = 2
    w_spec = pl.BlockSpec((1, width, per * part), lambda c: (0, 0, c))
    return pl.pallas_call(
        gate_up_kernel,
        grid=(n_rep // per,),
        in_specs=[pl.BlockSpec((rows, width), lambda c: (0, 0)), w_spec, w_spec],
        out_specs=pl.BlockSpec((per, rows, 2 * part), lambda c: (c, 0, 0)),
        out_shape=jax.ShapeDtypeStruct((n_rep, rows, 2 * part), F32),
        compiler_params=params(62),
        name="gate_up",
    )(x_rows, w_gate, w_up)


def hidden_kernel(offset, n_rep, me_ref, rows_ref, w_ref, *refs):
    part = w_ref.shape[1] // n_rep
    weights = w_ref[0, pl.ds(chunk_start(me_ref, offset, n_rep, part), part), :]
    total = lax.dot_general(rows_ref[...], weights, TRANS_B, preferred_element_type=F32)
    for arrived in refs[:-1]:
        total = total + arrived[...].astype(F32)
    refs[-1][...] = total.astype(refs[-1].dtype)


def hidden_term(me, dy_rows, w_down, n_rep, offset, arrived, dtype, name):
    rows = dy_rows.shape[0]
    part = w_down.shape[1] // n_rep
    return pl.pallas_call(
        lambda *refs: hidden_kernel(offset, n_rep, *refs),
        in_specs=[pl.BlockSpec(memory_space=pltpu.SMEM)] + [VMEM_SPEC] * (2 + len(arrived)),
        out_specs=VMEM_SPEC,
        out_shape=jax.ShapeDtypeStruct((rows, part), dtype),
        compiler_params=params(),
        name=name,
    )(me, dy_rows, w_down, *arrived)


def shift(rows, by):
    n_rep = lax.axis_size("rep")
    return lax.ppermute(rows, "rep", [(i, (i + by) % n_rep) for i in range(n_rep)])


def hidden_sums(me, dy_rows, w_down, n_rep):
    half = n_rep // 2
    up, down = (), ()
    for hop in range(half, 0, -1):
        term = hidden_term(me, dy_rows, w_down, n_rep, hop, up, BF16, "hidden_rise_%d" % hop)
        up = (shift(term, 1),)
        if hop < half:
            term = hidden_term(
                me, dy_rows, w_down, n_rep, n_rep - hop, down, BF16, "hidden_fall_%d" % hop
            )
            down = (shift(term, -1),)
    own = hidden_term(me, dy_rows, w_down, n_rep, 0, (), F32, "hidden_own")
    return own, up[0], down[0]


def activate_kernel(gu_ref, own_ref, up_ref, down_ref, out_ref):
    part = own_ref.shape[1]
    hidden = own_ref[...] + up_ref[...].astype(F32) + down_ref[...].astype(F32)
    gate = gu_ref[:, :part]
    up = gu_ref[:, part:]
    s = jax.nn.sigmoid(gate)
    out_ref[:, :part] = (hidden * up * s * (1.0 + gate * (1.0 - s))).astype(BF16)
    out_ref[:, part:] = (hidden * gate * s).astype(BF16)


def activate(gate_up, own, up, down):
    rows, part = own.shape
    block = rows // 2
    spec = pl.BlockSpec((block, part), lambda i: (i, 0))
    wide = pl.BlockSpec((block, 2 * part), lambda i: (i, 0))
    return pl.pallas_call(
        activate_kernel,
        grid=(rows // block,),
        in_specs=[wide, spec, spec, spec],
        out_specs=wide,
        out_shape=jax.ShapeDtypeStruct((rows, 2 * part), BF16),
        compiler_params=params(62),
        name="activate",
    )(gate_up, own, up, down)


def row_grad_kernel(offsets, has_start, n_rep, me_ref, *refs):
    blocks = refs[: len(offsets)]
    wg_ref, wu_ref = refs[len(offsets) : len(offsets) + 2]
    out_ref = refs[-1]
    total = refs[-2][...] if has_start else None
    for offset, block in zip(offsets, blocks):
        weights = chunk_weights(me_ref, offset, n_rep, wg_ref, wu_ref)
        term = lax.dot_general(block[...], weights, TRANS_B, preferred_element_type=F32)
        total = term if total is None else total + term
    out_ref[...] = total.astype(out_ref.dtype)


def row_grad(me, blocks, offsets, w_gate, w_up, n_rep, start, dtype, name):
    rows = blocks[0].shape[0]
    width = w_gate.shape[1]
    extra = () if start is None else (start,)
    return pl.pallas_call(
        lambda *refs: row_grad_kernel(offsets, start is not None, n_rep, *refs),
        in_specs=[pl.BlockSpec(memory_space=pltpu.SMEM)]
        + [VMEM_SPEC] * (len(blocks) + 2 + len(extra)),
        out_specs=VMEM_SPEC,
        out_shape=jax.ShapeDtypeStruct((rows, width), dtype),
        compiler_params=params(),
        name=name,
    )(me, *blocks, w_gate, w_up, *extra)


def gather_matmul(me, own, w_gate, w_up, n_rep):
    half = n_rep // 2
    blocks, offsets = [own], [0]
    up = down = own
    for step in range(1, half):
        up, down = shift(up, 1), shift(down, -1)
        blocks += [up, down]
        offsets += [n_rep - step, step]
    last = shift(up, 1)
    total = row_grad(me, blocks, offsets, w_gate, w_up, n_rep, None, F32, "row_grad_near")
    return row_grad(me, [last], [half], w_gate, w_up, n_rep, total, BF16, "row_grad_far")


def per_device(tokens, out_grad, expert_ids, route_weights, gate_weight, up_weight, down_weight):
    tok, width = tokens.shape
    top = expert_ids.shape[1]
    n_rep = lax.axis_size("rep")
    experts = lax.axis_size("outer") * lax.axis_size("local")
    capacity = max(2, 2 * tok * top // experts)
    slots = experts * capacity
    me = lax.axis_index("rep").astype(jnp.int32).reshape(1)
    send_dy, send_x, per_token_t = route(
        tokens, out_grad, expert_ids, route_weights, experts, capacity
    )

    def exchange(rows):
        blocks = rows.reshape(experts, capacity, width)
        return lax.all_to_all(blocks, ("outer", "local"), 0, 0, tiled=True).reshape(slots, width)

    x_rows = exchange(send_x)
    gate_up = lax.psum_scatter(
        gate_up_parts(x_rows, gate_weight, up_weight, n_rep), "rep", scatter_dimension=0
    )
    dy_rows = exchange(send_dy)
    own = activate(gate_up, *hidden_sums(me, dy_rows, down_weight, n_rep))
    returned = exchange(gather_matmul(me, own, gate_weight, up_weight, n_rep))
    return jnp.dot(per_token_t, returned, preferred_element_type=F32).astype(BF16)


def solution(mesh):
    return jax.shard_map(
        per_device,
        mesh=mesh,
        in_specs=(
            P(("outer", "local"), "rep"),
            P(("outer", "local"), "rep"),
            P(("outer", "local"), None),
            P(("outer", "local"), None),
            P(("outer", "local"), "rep", None),
            P(("outer", "local"), "rep", None),
            P(("outer", "local"), None, "rep"),
        ),
        out_specs=P(("outer", "local"), "rep"),
        check_vma=False,
    )
```

```python
import jax
import jax.numpy as jnp
from jax import lax
from jax.experimental import pallas as pl
from jax.experimental.pallas import tpu as pltpu
from jax.sharding import PartitionSpec as P

F32 = jnp.float32
BF16 = jnp.bfloat16
TRANS_B = (((1,), (1,)), ((), ()))
VMEM_SPEC = pl.BlockSpec(memory_space=pltpu.VMEM)


def params(mib=16):
    return pltpu.CompilerParams(vmem_limit_bytes=mib * 1024 * 1024)


def route_kernel(capacity, ids_hbm, w_hbm, tok_hbm, og_hbm, dy_ref, x_ref, pt_ref, *scratch):
    ids_ref, w_ref, tok_ref, og_ref, scaled_ref, sems = scratch
    copies = [
        pltpu.make_async_copy(src, dst, sems.at[n])
        for n, (src, dst) in enumerate(
            ((ids_hbm, ids_ref), (w_hbm, w_ref), (og_hbm, og_ref), (tok_hbm, tok_ref))
        )
    ]
    for copy in copies:
        copy.start()
    top, tok = ids_ref.shape
    rows = top * tok
    slots = dy_ref.shape[0]
    c_row = lax.broadcasted_iota(jnp.int32, (rows, tok), 0)
    pick_i = (c_row % tok == lax.broadcasted_iota(jnp.int32, (rows, tok), 1)).astype(BF16)
    c_k = lax.broadcasted_iota(jnp.int32, (rows, top), 0)
    pick_k = (c_k // tok == lax.broadcasted_iota(jnp.int32, (rows, top), 1)).astype(F32)
    sub = lax.broadcasted_iota(jnp.int32, (rows, rows), 0)
    lane = lax.broadcasted_iota(jnp.int32, (rows, rows), 1)
    order_sub = (sub % tok) * top + sub // tok
    order_lane = (lane % tok) * top + lane // tok
    for copy in copies:
        copy.wait()

    def column(values):
        spread = lax.dot_general(pick_i, values, TRANS_B, preferred_element_type=F32)
        return jnp.sum(spread * pick_k, axis=1, keepdims=True)

    ids_col = column(ids_ref[...].astype(F32).astype(BF16))
    w = w_ref[...]
    w_hi = w.astype(BF16)
    rest = w - w_hi.astype(F32)
    w_mid = rest.astype(BF16)
    w_lo = (rest - w_mid.astype(F32)).astype(BF16)
    w_col = column(w_hi) + (column(w_mid) + column(w_lo))
    ids_row = jnp.sum(jnp.where(sub == lane, ids_col, 0.0), axis=0, keepdims=True)
    earlier = (ids_col == ids_row) & (order_sub < order_lane)
    slot_row = jnp.sum(jnp.where(earlier, 1.0, 0.0), axis=0, keepdims=True)
    code = jnp.where(slot_row < capacity, ids_row * capacity + slot_row, -1.0).astype(jnp.int32)
    table = (lax.broadcasted_iota(jnp.int32, (slots, rows), 0) == code).astype(F32).astype(BF16)
    per_token = jnp.dot(table, pick_i, preferred_element_type=F32).astype(BF16)
    pt_ref[...] = lax.dot_general(
        pick_i, table, (((0,), (1,)), ((), ())), preferred_element_type=F32
    ).astype(BF16)
    og = jnp.dot(pick_i, og_ref[...], preferred_element_type=F32)
    scaled_ref[...] = (w_col * og).astype(BF16)
    x_ref[...] = jnp.dot(per_token, tok_ref[...], preferred_element_type=F32).astype(BF16)
    dy_ref[...] = jnp.dot(table, scaled_ref[...], preferred_element_type=F32).astype(BF16)


def route(tokens, out_grad, expert_ids, route_weights, experts, capacity):
    tok, width = tokens.shape
    top = expert_ids.shape[1]
    slots = experts * capacity
    return pl.pallas_call(
        lambda *refs: route_kernel(capacity, *refs),
        in_specs=[pl.BlockSpec(memory_space=pltpu.HBM)] * 4,
        out_specs=(VMEM_SPEC, VMEM_SPEC, VMEM_SPEC),
        out_shape=(
            jax.ShapeDtypeStruct((slots, width), BF16),
            jax.ShapeDtypeStruct((slots, width), BF16),
            jax.ShapeDtypeStruct((tok, slots), BF16),
        ),
        scratch_shapes=[
            pltpu.VMEM((top, tok), jnp.int32),
            pltpu.VMEM((top, tok), F32),
            pltpu.VMEM((tok, width), BF16),
            pltpu.VMEM((tok, width), BF16),
            pltpu.VMEM((tok * top, width), BF16),
            pltpu.SemaphoreType.DMA((4,)),
        ],
        compiler_params=params(63),
        name="route",
    )(expert_ids.T, route_weights.T, tokens, out_grad)


def chunk_start(me_ref, offset, n_rep, part):
    return pl.multiple_of(lax.rem(me_ref[0] + offset, n_rep) * part, part)


def chunk_weights(me_ref, offset, n_rep, wg_ref, wu_ref):
    part = wg_ref.shape[2] // n_rep
    cols = pl.ds(chunk_start(me_ref, offset, n_rep, part), part)
    return jnp.concatenate([wg_ref[0, :, cols], wu_ref[0, :, cols]], axis=1)


def gate_up_kernel(x_ref, wg_ref, wu_ref, out_ref):
    per = out_ref.shape[0]
    part = wg_ref.shape[2] // per
    for j in range(per):
        cols = slice(j * part, (j + 1) * part)
        weights = jnp.concatenate([wg_ref[0, :, cols], wu_ref[0, :, cols]], axis=1)
        out_ref[j] = jnp.dot(x_ref[...], weights, preferred_element_type=F32)


def gate_up_parts(x_rows, w_gate, w_up, n_rep):
    rows, width = x_rows.shape
    part = w_gate.shape[2] // n_rep
    per = 2
    w_spec = pl.BlockSpec((1, width, per * part), lambda c: (0, 0, c))
    return pl.pallas_call(
        gate_up_kernel,
        grid=(n_rep // per,),
        in_specs=[pl.BlockSpec((rows, width), lambda c: (0, 0)), w_spec, w_spec],
        out_specs=pl.BlockSpec((per, rows, 2 * part), lambda c: (c, 0, 0)),
        out_shape=jax.ShapeDtypeStruct((n_rep, rows, 2 * part), F32),
        compiler_params=params(62),
        name="gate_up",
    )(x_rows, w_gate, w_up)


def hidden_kernel(offset, n_rep, me_ref, rows_ref, w_ref, *refs):
    part = w_ref.shape[1] // n_rep
    weights = w_ref[0, pl.ds(chunk_start(me_ref, offset, n_rep, part), part), :]
    total = lax.dot_general(rows_ref[...], weights, TRANS_B, preferred_element_type=F32)
    for arrived in refs[:-1]:
        total = total + arrived[...].astype(F32)
    refs[-1][...] = total.astype(refs[-1].dtype)


def hidden_term(me, dy_rows, w_down, n_rep, offset, arrived, dtype, name):
    rows = dy_rows.shape[0]
    part = w_down.shape[1] // n_rep
    return pl.pallas_call(
        lambda *refs: hidden_kernel(offset, n_rep, *refs),
        in_specs=[pl.BlockSpec(memory_space=pltpu.SMEM)] + [VMEM_SPEC] * (2 + len(arrived)),
        out_specs=VMEM_SPEC,
        out_shape=jax.ShapeDtypeStruct((rows, part), dtype),
        compiler_params=params(),
        name=name,
    )(me, dy_rows, w_down, *arrived)


def shift(rows, by):
    n_rep = lax.axis_size("rep")
    return lax.ppermute(rows, "rep", [(i, (i + by) % n_rep) for i in range(n_rep)])


def hidden_sums(me, dy_rows, w_down, n_rep):
    def term(offset, arrived, dtype, name):
        return hidden_term(me, dy_rows, w_down, n_rep, offset % n_rep, arrived, dtype, name)

    near = min(2, n_rep // 2 - 1)
    up, down = (), ()
    for hop in range(near, 0, -1):
        up = (shift(term(hop, up, BF16, "hidden_rise_%d" % hop), 1),)
        down = (shift(term(-hop, down, BF16, "hidden_fall_%d" % hop), -1),)
    straight = tuple(
        shift(term(far, (), BF16, "hidden_far_%d" % far), far)
        for far in range(near + 1, n_rep - near)
    )
    return (term(0, (), F32, "hidden_own"),) + up + down + straight


def activate_kernel(gu_ref, own_ref, *refs):
    part = own_ref.shape[1]
    out_ref = refs[-1]
    hidden = own_ref[...]
    for arrived in refs[:-1]:
        hidden = hidden + arrived[...].astype(F32)
    gate = gu_ref[:, :part]
    up = gu_ref[:, part:]
    s = jax.nn.sigmoid(gate)
    out_ref[:, :part] = (hidden * up * s * (1.0 + gate * (1.0 - s))).astype(BF16)
    out_ref[:, part:] = (hidden * gate * s).astype(BF16)


def activate(gate_up, own, *arrived):
    rows, part = own.shape
    block = rows // 2
    spec = pl.BlockSpec((block, part), lambda i: (i, 0))
    wide = pl.BlockSpec((block, 2 * part), lambda i: (i, 0))
    return pl.pallas_call(
        activate_kernel,
        grid=(rows // block,),
        in_specs=[wide, spec] + [spec] * len(arrived),
        out_specs=wide,
        out_shape=jax.ShapeDtypeStruct((rows, 2 * part), BF16),
        compiler_params=params(62),
        name="activate",
    )(gate_up, own, *arrived)


def row_grad_kernel(offsets, has_start, n_rep, me_ref, *refs):
    blocks = refs[: len(offsets)]
    wg_ref, wu_ref = refs[len(offsets) : len(offsets) + 2]
    out_ref = refs[-1]
    total = refs[-2][...] if has_start else None
    for offset, block in zip(offsets, blocks):
        weights = chunk_weights(me_ref, offset, n_rep, wg_ref, wu_ref)
        term = lax.dot_general(block[...], weights, TRANS_B, preferred_element_type=F32)
        total = term if total is None else total + term
    out_ref[...] = total.astype(out_ref.dtype)


def row_grad(me, blocks, offsets, w_gate, w_up, n_rep, start, dtype, name):
    rows = blocks[0].shape[0]
    width = w_gate.shape[1]
    extra = () if start is None else (start,)
    return pl.pallas_call(
        lambda *refs: row_grad_kernel(offsets, start is not None, n_rep, *refs),
        in_specs=[pl.BlockSpec(memory_space=pltpu.SMEM)]
        + [VMEM_SPEC] * (len(blocks) + 2 + len(extra)),
        out_specs=VMEM_SPEC,
        out_shape=jax.ShapeDtypeStruct((rows, width), dtype),
        compiler_params=params(),
        name=name,
    )(me, *blocks, w_gate, w_up, *extra)


def gather_matmul(me, own, w_gate, w_up, n_rep):
    half = n_rep // 2
    blocks, offsets = [own], [0]
    up = down = own
    far = shift(own, half)
    for step in range(1, half):
        up, down = shift(up, 1), shift(down, -1)
        blocks += [up, down]
        offsets += [n_rep - step, step]
    total = row_grad(
        me, blocks[:-2], offsets[:-2], w_gate, w_up, n_rep, None, F32, "row_grad_near"
    )
    blocks, offsets = blocks[-2:] + [far], offsets[-2:] + [half]
    return row_grad(me, blocks, offsets, w_gate, w_up, n_rep, total, BF16, "row_grad_far")


def per_device(tokens, out_grad, expert_ids, route_weights, gate_weight, up_weight, down_weight):
    tok, width = tokens.shape
    top = expert_ids.shape[1]
    n_rep = lax.axis_size("rep")
    experts = lax.axis_size("outer") * lax.axis_size("local")
    capacity = max(2, 2 * tok * top // experts)
    slots = experts * capacity
    me = lax.axis_index("rep").astype(jnp.int32).reshape(1)
    send_dy, send_x, per_token_t = route(
        tokens, out_grad, expert_ids, route_weights, experts, capacity
    )

    def exchange(rows):
        blocks = rows.reshape(experts, capacity, width)
        return lax.all_to_all(blocks, ("outer", "local"), 0, 0, tiled=True).reshape(slots, width)

    x_rows = exchange(send_x)
    gate_up = lax.psum_scatter(
        gate_up_parts(x_rows, gate_weight, up_weight, n_rep), "rep", scatter_dimension=0
    )
    dy_rows = exchange(send_dy)
    own = activate(gate_up, *hidden_sums(me, dy_rows, down_weight, n_rep))
    returned = exchange(gather_matmul(me, own, gate_weight, up_weight, n_rep))
    return jnp.dot(per_token_t, returned, preferred_element_type=F32).astype(BF16)


def solution(mesh):
    return jax.shard_map(
        per_device,
        mesh=mesh,
        in_specs=(
            P(("outer", "local"), "rep"),
            P(("outer", "local"), "rep"),
            P(("outer", "local"), None),
            P(("outer", "local"), None),
            P(("outer", "local"), "rep", None),
            P(("outer", "local"), "rep", None),
            P(("outer", "local"), None, "rep"),
        ),
        out_specs=P(("outer", "local"), "rep"),
        check_vma=False,
    )
```

```python
import jax
import jax.numpy as jnp
from jax import lax
from jax.experimental import pallas as pl
from jax.experimental.pallas import tpu as pltpu
from jax.sharding import PartitionSpec as P

F32 = jnp.float32
BF16 = jnp.bfloat16
TRANS_B = (((1,), (1,)), ((), ()))
VMEM_SPEC = pl.BlockSpec(memory_space=pltpu.VMEM)


def params(mib=16):
    return pltpu.CompilerParams(vmem_limit_bytes=mib * 1024 * 1024)


def route_kernel(capacity, ids_hbm, w_hbm, tok_hbm, og_hbm, send_ref, pt_ref, *scratch):
    ids_ref, w_ref, tok_ref, og_ref, scaled_ref, sems = scratch
    copies = [
        pltpu.make_async_copy(src, dst, sems.at[n])
        for n, (src, dst) in enumerate(
            ((ids_hbm, ids_ref), (w_hbm, w_ref), (og_hbm, og_ref), (tok_hbm, tok_ref))
        )
    ]
    for copy in copies:
        copy.start()
    top, tok = ids_ref.shape
    width = tok_ref.shape[1]
    rows = top * tok
    slots = send_ref.shape[0]
    c_row = lax.broadcasted_iota(jnp.int32, (rows, tok), 0)
    pick_i = (c_row % tok == lax.broadcasted_iota(jnp.int32, (rows, tok), 1)).astype(BF16)
    c_k = lax.broadcasted_iota(jnp.int32, (rows, top), 0)
    pick_k = (c_k // tok == lax.broadcasted_iota(jnp.int32, (rows, top), 1)).astype(F32)
    sub = lax.broadcasted_iota(jnp.int32, (rows, rows), 0)
    lane = lax.broadcasted_iota(jnp.int32, (rows, rows), 1)
    order_sub = (sub % tok) * top + sub // tok
    order_lane = (lane % tok) * top + lane // tok
    for copy in copies:
        copy.wait()

    def column(values):
        spread = lax.dot_general(pick_i, values, TRANS_B, preferred_element_type=F32)
        return jnp.sum(spread * pick_k, axis=1, keepdims=True)

    ids_col = column(ids_ref[...].astype(F32).astype(BF16))
    w = w_ref[...]
    w_hi = w.astype(BF16)
    rest = w - w_hi.astype(F32)
    w_mid = rest.astype(BF16)
    w_lo = (rest - w_mid.astype(F32)).astype(BF16)
    w_col = column(w_hi) + (column(w_mid) + column(w_lo))
    ids_row = jnp.sum(jnp.where(sub == lane, ids_col, 0.0), axis=0, keepdims=True)
    earlier = (ids_col == ids_row) & (order_sub < order_lane)
    slot_row = jnp.sum(jnp.where(earlier, 1.0, 0.0), axis=0, keepdims=True)
    code = jnp.where(slot_row < capacity, ids_row * capacity + slot_row, -1.0).astype(jnp.int32)
    table = (lax.broadcasted_iota(jnp.int32, (slots, rows), 0) == code).astype(F32).astype(BF16)
    per_token = jnp.dot(table, pick_i, preferred_element_type=F32).astype(BF16)
    pt_ref[...] = lax.dot_general(
        pick_i, table, (((0,), (1,)), ((), ())), preferred_element_type=F32
    ).astype(BF16)
    og = jnp.dot(pick_i, og_ref[...], preferred_element_type=F32)
    scaled_ref[...] = (w_col * og).astype(BF16)
    send_ref[:, :width] = jnp.dot(
        per_token, tok_ref[...], preferred_element_type=F32
    ).astype(BF16)
    send_ref[:, width:] = jnp.dot(
        table, scaled_ref[...], preferred_element_type=F32
    ).astype(BF16)


def route(tokens, out_grad, expert_ids, route_weights, experts, capacity):
    tok, width = tokens.shape
    top = expert_ids.shape[1]
    slots = experts * capacity
    return pl.pallas_call(
        lambda *refs: route_kernel(capacity, *refs),
        in_specs=[pl.BlockSpec(memory_space=pltpu.HBM)] * 4,
        out_specs=(VMEM_SPEC, VMEM_SPEC),
        out_shape=(
            jax.ShapeDtypeStruct((slots, 2 * width), BF16),
            jax.ShapeDtypeStruct((tok, slots), BF16),
        ),
        scratch_shapes=[
            pltpu.VMEM((top, tok), jnp.int32),
            pltpu.VMEM((top, tok), F32),
            pltpu.VMEM((tok, width), BF16),
            pltpu.VMEM((tok, width), BF16),
            pltpu.VMEM((tok * top, width), BF16),
            pltpu.SemaphoreType.DMA((4,)),
        ],
        compiler_params=params(63),
        name="route",
    )(expert_ids.T, route_weights.T, tokens, out_grad)


def chunk_start(me_ref, offset, n_rep, part):
    return pl.multiple_of(lax.rem(me_ref[0] + offset, n_rep) * part, part)


def chunk_weights(me_ref, offset, n_rep, wg_ref, wu_ref):
    part = wg_ref.shape[2] // n_rep
    cols = pl.ds(chunk_start(me_ref, offset, n_rep, part), part)
    return jnp.concatenate([wg_ref[0, :, cols], wu_ref[0, :, cols]], axis=1)


def term_kernel(offset, n_rep, me_ref, rows_ref, wg_ref, wu_ref, wd_ref, *refs):
    out_ref = refs[-1]
    width = wg_ref.shape[1]
    part = wg_ref.shape[2] // n_rep
    weights = chunk_weights(me_ref, offset, n_rep, wg_ref, wu_ref)
    down = wd_ref[0, pl.ds(chunk_start(me_ref, offset, n_rep, part), part), :]
    gate_up = jnp.dot(rows_ref[:, :width], weights, preferred_element_type=F32)
    hidden = lax.dot_general(rows_ref[:, width:], down, TRANS_B, preferred_element_type=F32)
    for arrived in refs[:-1]:
        gate_up = gate_up + arrived[:, : 2 * part].astype(F32)
        hidden = hidden + arrived[:, 2 * part :].astype(F32)
    out_ref[:, : 2 * part] = gate_up.astype(out_ref.dtype)
    out_ref[:, 2 * part :] = hidden.astype(out_ref.dtype)


def shift(rows, by):
    n_rep = lax.axis_size("rep")
    return lax.ppermute(rows, "rep", [(i, (i + by) % n_rep) for i in range(n_rep)])


def width_sums(me, both_rows, w_gate, w_up, w_down, n_rep):
    rows = both_rows.shape[0]
    part = w_gate.shape[2] // n_rep

    def term(offset, arrived, dtype, name):
        return pl.pallas_call(
            lambda *refs: term_kernel(offset, n_rep, *refs),
            in_specs=[pl.BlockSpec(memory_space=pltpu.SMEM)] + [VMEM_SPEC] * (4 + len(arrived)),
            out_specs=VMEM_SPEC,
            out_shape=jax.ShapeDtypeStruct((rows, 3 * part), dtype),
            compiler_params=params(),
            name=name,
        )(me, both_rows, w_gate, w_up, w_down, *arrived)

    half = n_rep // 2
    up, down = (), ()
    for hop in range(half, 0, -1):
        up = (shift(term(hop, up, BF16, "rise_%d" % hop), 1),)
        if hop < half:
            down = (shift(term(n_rep - hop, down, BF16, "fall_%d" % hop), -1),)
    return term(0, (), F32, "own_term"), up[0], down[0]


def activate_kernel(own_ref, up_ref, down_ref, out_ref):
    part = own_ref.shape[1] // 3
    sums = own_ref[...] + up_ref[...].astype(F32) + down_ref[...].astype(F32)
    gate = sums[:, :part]
    up = sums[:, part : 2 * part]
    hidden = sums[:, 2 * part :]
    s = jax.nn.sigmoid(gate)
    out_ref[:, :part] = (hidden * up * s * (1.0 + gate * (1.0 - s))).astype(BF16)
    out_ref[:, part:] = (hidden * gate * s).astype(BF16)


def activate(own, up, down):
    rows, part3 = own.shape
    return pl.pallas_call(
        activate_kernel,
        in_specs=[VMEM_SPEC] * 3,
        out_specs=VMEM_SPEC,
        out_shape=jax.ShapeDtypeStruct((rows, part3 // 3 * 2), BF16),
        compiler_params=params(),
        name="activate",
    )(own, up, down)


def row_grad_kernel(offsets, has_start, n_rep, me_ref, *refs):
    blocks = refs[: len(offsets)]
    wg_ref, wu_ref = refs[len(offsets) : len(offsets) + 2]
    out_ref = refs[-1]
    total = refs[-2][...] if has_start else None
    for offset, block in zip(offsets, blocks):
        weights = chunk_weights(me_ref, offset, n_rep, wg_ref, wu_ref)
        term = lax.dot_general(block[...], weights, TRANS_B, preferred_element_type=F32)
        total = term if total is None else total + term
    out_ref[...] = total.astype(out_ref.dtype)


def row_grad(me, blocks, offsets, w_gate, w_up, n_rep, start, dtype, name):
    rows = blocks[0].shape[0]
    width = w_gate.shape[1]
    extra = () if start is None else (start,)
    return pl.pallas_call(
        lambda *refs: row_grad_kernel(offsets, start is not None, n_rep, *refs),
        in_specs=[pl.BlockSpec(memory_space=pltpu.SMEM)]
        + [VMEM_SPEC] * (len(blocks) + 2 + len(extra)),
        out_specs=VMEM_SPEC,
        out_shape=jax.ShapeDtypeStruct((rows, width), dtype),
        compiler_params=params(),
        name=name,
    )(me, *blocks, w_gate, w_up, *extra)


def gather_matmul(me, own, w_gate, w_up, n_rep):
    half = n_rep // 2
    blocks, offsets = [own], [0]
    up = down = own
    for step in range(1, half):
        up, down = shift(up, 1), shift(down, -1)
        blocks += [up, down]
        offsets += [n_rep - step, step]
    last = shift(up, 1)
    total = row_grad(me, blocks, offsets, w_gate, w_up, n_rep, None, F32, "row_grad_near")
    return row_grad(me, [last], [half], w_gate, w_up, n_rep, total, BF16, "row_grad_far")


def per_device(tokens, out_grad, expert_ids, route_weights, gate_weight, up_weight, down_weight):
    tok, width = tokens.shape
    top = expert_ids.shape[1]
    n_rep = lax.axis_size("rep")
    experts = lax.axis_size("outer") * lax.axis_size("local")
    capacity = max(2, 2 * tok * top // experts)
    slots = experts * capacity
    me = lax.axis_index("rep").astype(jnp.int32).reshape(1)
    send, per_token_t = route(tokens, out_grad, expert_ids, route_weights, experts, capacity)

    def exchange(rows):
        blocks = rows.reshape(experts, capacity, rows.shape[1])
        return lax.all_to_all(blocks, ("outer", "local"), 0, 0, tiled=True).reshape(rows.shape)

    both_rows = exchange(send)
    own = activate(
        *width_sums(me, both_rows, gate_weight, up_weight, down_weight, n_rep)
    )
    returned = exchange(gather_matmul(me, own, gate_weight, up_weight, n_rep))
    return jnp.dot(per_token_t, returned, preferred_element_type=F32).astype(BF16)


def solution(mesh):
    return jax.shard_map(
        per_device,
        mesh=mesh,
        in_specs=(
            P(("outer", "local"), "rep"),
            P(("outer", "local"), "rep"),
            P(("outer", "local"), None),
            P(("outer", "local"), None),
            P(("outer", "local"), "rep", None),
            P(("outer", "local"), "rep", None),
            P(("outer", "local"), None, "rep"),
        ),
        out_specs=P(("outer", "local"), "rep"),
        check_vma=False,
    )
```

```python
import jax
import jax.numpy as jnp
from jax import lax
from jax.experimental import pallas as pl
from jax.experimental.pallas import tpu as pltpu
from jax.sharding import PartitionSpec as P

F32 = jnp.float32
BF16 = jnp.bfloat16
TRANS_B = (((1,), (1,)), ((), ()))
VMEM_SPEC = pl.BlockSpec(memory_space=pltpu.VMEM)


def params(mib=16):
    return pltpu.CompilerParams(vmem_limit_bytes=mib * 1024 * 1024)


def route_kernel(capacity, ids_hbm, w_hbm, tok_hbm, og_hbm, send_ref, pt_ref, *scratch):
    ids_ref, w_ref, tok_ref, og_ref, scaled_ref, sems = scratch
    copies = [
        pltpu.make_async_copy(src, dst, sems.at[n])
        for n, (src, dst) in enumerate(
            ((ids_hbm, ids_ref), (w_hbm, w_ref), (og_hbm, og_ref), (tok_hbm, tok_ref))
        )
    ]
    for copy in copies:
        copy.start()
    top, tok = ids_ref.shape
    width = tok_ref.shape[1]
    rows = top * tok
    slots = pt_ref.shape[1]
    c_row = lax.broadcasted_iota(jnp.int32, (rows, tok), 0)
    pick_i = (c_row % tok == lax.broadcasted_iota(jnp.int32, (rows, tok), 1)).astype(BF16)
    c_k = lax.broadcasted_iota(jnp.int32, (rows, top), 0)
    pick_k = (c_k // tok == lax.broadcasted_iota(jnp.int32, (rows, top), 1)).astype(F32)
    sub = lax.broadcasted_iota(jnp.int32, (rows, rows), 0)
    lane = lax.broadcasted_iota(jnp.int32, (rows, rows), 1)
    order_sub = (sub % tok) * top + sub // tok
    order_lane = (lane % tok) * top + lane // tok
    for copy in copies:
        copy.wait()

    def column(values):
        spread = lax.dot_general(pick_i, values, TRANS_B, preferred_element_type=F32)
        return jnp.sum(spread * pick_k, axis=1, keepdims=True)

    ids_col = column(ids_ref[...].astype(F32).astype(BF16))
    w = w_ref[...]
    w_hi = w.astype(BF16)
    rest = w - w_hi.astype(F32)
    w_mid = rest.astype(BF16)
    w_lo = (rest - w_mid.astype(F32)).astype(BF16)
    w_col = column(w_hi) + (column(w_mid) + column(w_lo))
    ids_row = jnp.sum(jnp.where(sub == lane, ids_col, 0.0), axis=0, keepdims=True)
    earlier = (ids_col == ids_row) & (order_sub < order_lane)
    slot_row = jnp.sum(jnp.where(earlier, 1.0, 0.0), axis=0, keepdims=True)
    kept = slot_row < capacity

    def table(size, stride, offset):
        code = jnp.where(kept, ids_row * stride + slot_row + offset, -1.0).astype(jnp.int32)
        slot = lax.broadcasted_iota(jnp.int32, (size, rows), 0)
        return (slot == code).astype(F32).astype(BF16)

    pt_ref[...] = lax.dot_general(
        pick_i,
        table(slots, capacity, 0),
        (((0,), (1,)), ((), ())),
        preferred_element_type=F32,
    ).astype(BF16)
    og = jnp.dot(pick_i, og_ref[...], preferred_element_type=F32)
    scaled_ref[...] = (w_col * og).astype(BF16)
    for_x = table(2 * slots, 2 * capacity, 0)
    per_token = jnp.dot(for_x, pick_i, preferred_element_type=F32).astype(BF16)
    for_dy = table(2 * slots, 2 * capacity, capacity)
    send_ref[...] = (
        jnp.dot(per_token, tok_ref[...], preferred_element_type=F32)
        + jnp.dot(for_dy, scaled_ref[...], preferred_element_type=F32)
    ).astype(BF16)


def route(tokens, out_grad, expert_ids, route_weights, experts, capacity):
    tok, width = tokens.shape
    top = expert_ids.shape[1]
    slots = experts * capacity
    return pl.pallas_call(
        lambda *refs: route_kernel(capacity, *refs),
        in_specs=[pl.BlockSpec(memory_space=pltpu.HBM)] * 4,
        out_specs=(VMEM_SPEC, VMEM_SPEC),
        out_shape=(
            jax.ShapeDtypeStruct((2 * slots, width), BF16),
            jax.ShapeDtypeStruct((tok, slots), BF16),
        ),
        scratch_shapes=[
            pltpu.VMEM((top, tok), jnp.int32),
            pltpu.VMEM((top, tok), F32),
            pltpu.VMEM((tok, width), BF16),
            pltpu.VMEM((tok, width), BF16),
            pltpu.VMEM((tok * top, width), BF16),
            pltpu.SemaphoreType.DMA((4,)),
        ],
        compiler_params=params(63),
        name="route",
    )(expert_ids.T, route_weights.T, tokens, out_grad)


def split_kernel(capacity, in_ref, out_ref):
    width = in_ref.shape[1]
    block = 32 * capacity
    rows = block // 2
    r = lax.broadcasted_iota(jnp.int32, (rows, block), 0)
    place = (r // capacity) * (2 * capacity) + r % capacity
    lane = lax.broadcasted_iota(jnp.int32, (rows, block), 1)
    for half in range(2):
        pick = (lane == place + half * capacity).astype(F32).astype(BF16)
        for b in range(in_ref.shape[0] // block):
            out_ref[b * rows : (b + 1) * rows, half * width : (half + 1) * width] = jnp.dot(
                pick, in_ref[b * block : (b + 1) * block, :], preferred_element_type=F32
            ).astype(BF16)


def split(received, capacity):
    rows, width = received.shape
    return pl.pallas_call(
        lambda *refs: split_kernel(capacity, *refs),
        in_specs=[VMEM_SPEC],
        out_specs=VMEM_SPEC,
        out_shape=jax.ShapeDtypeStruct((rows // 2, 2 * width), BF16),
        compiler_params=params(),
        name="split",
    )(received)


def chunk_start(me_ref, offset, n_rep, part):
    return pl.multiple_of(lax.rem(me_ref[0] + offset, n_rep) * part, part)


def chunk_weights(me_ref, offset, n_rep, wg_ref, wu_ref):
    part = wg_ref.shape[2] // n_rep
    cols = pl.ds(chunk_start(me_ref, offset, n_rep, part), part)
    return jnp.concatenate([wg_ref[0, :, cols], wu_ref[0, :, cols]], axis=1)


def term_kernel(offset, n_rep, me_ref, rows_ref, wg_ref, wu_ref, wd_ref, *refs):
    out_ref = refs[-1]
    width = wg_ref.shape[1]
    part = wg_ref.shape[2] // n_rep
    weights = chunk_weights(me_ref, offset, n_rep, wg_ref, wu_ref)
    down = wd_ref[0, pl.ds(chunk_start(me_ref, offset, n_rep, part), part), :]
    gate_up = jnp.dot(rows_ref[:, :width], weights, preferred_element_type=F32)
    hidden = lax.dot_general(rows_ref[:, width:], down, TRANS_B, preferred_element_type=F32)
    for arrived in refs[:-1]:
        gate_up = gate_up + arrived[:, : 2 * part].astype(F32)
        hidden = hidden + arrived[:, 2 * part :].astype(F32)
    out_ref[:, : 2 * part] = gate_up.astype(out_ref.dtype)
    out_ref[:, 2 * part :] = hidden.astype(out_ref.dtype)


def shift(rows, by):
    n_rep = lax.axis_size("rep")
    return lax.ppermute(rows, "rep", [(i, (i + by) % n_rep) for i in range(n_rep)])


def width_sums(me, both_rows, w_gate, w_up, w_down, n_rep):
    rows = both_rows.shape[0]
    part = w_gate.shape[2] // n_rep

    def term(offset, arrived, dtype, name):
        return pl.pallas_call(
            lambda *refs: term_kernel(offset, n_rep, *refs),
            in_specs=[pl.BlockSpec(memory_space=pltpu.SMEM)] + [VMEM_SPEC] * (4 + len(arrived)),
            out_specs=VMEM_SPEC,
            out_shape=jax.ShapeDtypeStruct((rows, 3 * part), dtype),
            compiler_params=params(),
            name=name,
        )(me, both_rows, w_gate, w_up, w_down, *arrived)

    half = n_rep // 2
    up, down = (), ()
    for hop in range(half, 0, -1):
        up = (shift(term(hop, up, BF16, "rise_%d" % hop), 1),)
        if hop < half:
            down = (shift(term(n_rep - hop, down, BF16, "fall_%d" % hop), -1),)
    return term(0, (), F32, "own_term"), up[0], down[0]


def activate_kernel(own_ref, up_ref, down_ref, out_ref):
    part = own_ref.shape[1] // 3
    sums = own_ref[...] + up_ref[...].astype(F32) + down_ref[...].astype(F32)
    gate = sums[:, :part]
    up = sums[:, part : 2 * part]
    hidden = sums[:, 2 * part :]
    s = jax.nn.sigmoid(gate)
    out_ref[:, :part] = (hidden * up * s * (1.0 + gate * (1.0 - s))).astype(BF16)
    out_ref[:, part:] = (hidden * gate * s).astype(BF16)


def activate(own, up, down):
    rows, part3 = own.shape
    return pl.pallas_call(
        activate_kernel,
        in_specs=[VMEM_SPEC] * 3,
        out_specs=VMEM_SPEC,
        out_shape=jax.ShapeDtypeStruct((rows, part3 // 3 * 2), BF16),
        compiler_params=params(),
        name="activate",
    )(own, up, down)


def row_grad_kernel(offsets, has_start, n_rep, me_ref, *refs):
    blocks = refs[: len(offsets)]
    wg_ref, wu_ref = refs[len(offsets) : len(offsets) + 2]
    out_ref = refs[-1]
    total = refs[-2][...] if has_start else None
    for offset, block in zip(offsets, blocks):
        weights = chunk_weights(me_ref, offset, n_rep, wg_ref, wu_ref)
        term = lax.dot_general(block[...], weights, TRANS_B, preferred_element_type=F32)
        total = term if total is None else total + term
    out_ref[...] = total.astype(out_ref.dtype)


def row_grad(me, blocks, offsets, w_gate, w_up, n_rep, start, dtype, name):
    rows = blocks[0].shape[0]
    width = w_gate.shape[1]
    extra = () if start is None else (start,)
    return pl.pallas_call(
        lambda *refs: row_grad_kernel(offsets, start is not None, n_rep, *refs),
        in_specs=[pl.BlockSpec(memory_space=pltpu.SMEM)]
        + [VMEM_SPEC] * (len(blocks) + 2 + len(extra)),
        out_specs=VMEM_SPEC,
        out_shape=jax.ShapeDtypeStruct((rows, width), dtype),
        compiler_params=params(),
        name=name,
    )(me, *blocks, w_gate, w_up, *extra)


def gather_matmul(me, own, w_gate, w_up, n_rep):
    half = n_rep // 2
    blocks, offsets = [own], [0]
    up = down = own
    for step in range(1, half):
        up, down = shift(up, 1), shift(down, -1)
        blocks += [up, down]
        offsets += [n_rep - step, step]
    last = shift(up, 1)
    total = row_grad(me, blocks, offsets, w_gate, w_up, n_rep, None, F32, "row_grad_near")
    return row_grad(me, [last], [half], w_gate, w_up, n_rep, total, BF16, "row_grad_far")


def per_device(tokens, out_grad, expert_ids, route_weights, gate_weight, up_weight, down_weight):
    tok, width = tokens.shape
    top = expert_ids.shape[1]
    n_rep = lax.axis_size("rep")
    experts = lax.axis_size("outer") * lax.axis_size("local")
    capacity = max(2, 2 * tok * top // experts)
    slots = experts * capacity
    me = lax.axis_index("rep").astype(jnp.int32).reshape(1)
    send, per_token_t = route(tokens, out_grad, expert_ids, route_weights, experts, capacity)

    def exchange(rows):
        blocks = rows.reshape(experts, rows.shape[0] // experts, width)
        return lax.all_to_all(blocks, ("outer", "local"), 0, 0, tiled=True).reshape(rows.shape)

    both_rows = split(exchange(send), capacity)
    own = activate(
        *width_sums(me, both_rows, gate_weight, up_weight, down_weight, n_rep)
    )
    returned = exchange(gather_matmul(me, own, gate_weight, up_weight, n_rep))
    return jnp.dot(per_token_t, returned, preferred_element_type=F32).astype(BF16)


def solution(mesh):
    return jax.shard_map(
        per_device,
        mesh=mesh,
        in_specs=(
            P(("outer", "local"), "rep"),
            P(("outer", "local"), "rep"),
            P(("outer", "local"), None),
            P(("outer", "local"), None),
            P(("outer", "local"), "rep", None),
            P(("outer", "local"), "rep", None),
            P(("outer", "local"), None, "rep"),
        ),
        out_specs=P(("outer", "local"), "rep"),
        check_vma=False,
    )
```

```python
import jax
import jax.numpy as jnp
from jax import lax
from jax.experimental import pallas as pl
from jax.experimental.pallas import tpu as pltpu
from jax.sharding import PartitionSpec as P

F32 = jnp.float32
BF16 = jnp.bfloat16
TRANS_B = (((1,), (1,)), ((), ()))
VMEM_SPEC = pl.BlockSpec(memory_space=pltpu.VMEM)


def params(mib=16):
    return pltpu.CompilerParams(vmem_limit_bytes=mib * 1024 * 1024)


def route_kernel(capacity, ids_hbm, w_hbm, tok_hbm, og_hbm, send_ref, pt_ref, *scratch):
    ids_ref, w_ref, tok_ref, og_ref, scaled_ref, sems = scratch
    copies = [
        pltpu.make_async_copy(src, dst, sems.at[n])
        for n, (src, dst) in enumerate(
            ((ids_hbm, ids_ref), (w_hbm, w_ref), (og_hbm, og_ref), (tok_hbm, tok_ref))
        )
    ]
    for copy in copies:
        copy.start()
    top, tok = ids_ref.shape
    width = tok_ref.shape[1]
    rows = top * tok
    slots = pt_ref.shape[1]
    c_row = lax.broadcasted_iota(jnp.int32, (rows, tok), 0)
    pick_i = (c_row % tok == lax.broadcasted_iota(jnp.int32, (rows, tok), 1)).astype(BF16)
    c_k = lax.broadcasted_iota(jnp.int32, (rows, top), 0)
    pick_k = (c_k // tok == lax.broadcasted_iota(jnp.int32, (rows, top), 1)).astype(F32)
    sub = lax.broadcasted_iota(jnp.int32, (rows, rows), 0)
    lane = lax.broadcasted_iota(jnp.int32, (rows, rows), 1)
    order_sub = (sub % tok) * top + sub // tok
    order_lane = (lane % tok) * top + lane // tok
    for copy in copies:
        copy.wait()

    def column(values):
        spread = lax.dot_general(pick_i, values, TRANS_B, preferred_element_type=F32)
        return jnp.sum(spread * pick_k, axis=1, keepdims=True)

    ids_col = column(ids_ref[...].astype(F32).astype(BF16))
    w = w_ref[...]
    w_hi = w.astype(BF16)
    rest = w - w_hi.astype(F32)
    w_mid = rest.astype(BF16)
    w_lo = (rest - w_mid.astype(F32)).astype(BF16)
    w_col = column(w_hi) + (column(w_mid) + column(w_lo))
    ids_row = jnp.sum(jnp.where(sub == lane, ids_col, 0.0), axis=0, keepdims=True)
    earlier = (ids_col == ids_row) & (order_sub < order_lane)
    slot_row = jnp.sum(jnp.where(earlier, 1.0, 0.0), axis=0, keepdims=True)
    kept = slot_row < capacity

    def table(size, stride, offset):
        code = jnp.where(kept, ids_row * stride + slot_row + offset, -1.0).astype(jnp.int32)
        slot = lax.broadcasted_iota(jnp.int32, (size, rows), 0)
        return (slot == code).astype(F32).astype(BF16)

    pt_ref[...] = lax.dot_general(
        pick_i,
        table(slots, capacity, 0),
        (((0,), (1,)), ((), ())),
        preferred_element_type=F32,
    ).astype(BF16)
    og = jnp.dot(pick_i, og_ref[...], preferred_element_type=F32)
    scaled_ref[...] = (w_col * og).astype(BF16)
    for_x = table(2 * slots, 2 * capacity, 0)
    per_token = jnp.dot(for_x, pick_i, preferred_element_type=F32).astype(BF16)
    for_dy = table(2 * slots, 2 * capacity, capacity)
    send_ref[...] = (
        jnp.dot(per_token, tok_ref[...], preferred_element_type=F32)
        + jnp.dot(for_dy, scaled_ref[...], preferred_element_type=F32)
    ).astype(BF16)


def route(tokens, out_grad, expert_ids, route_weights, experts, capacity):
    tok, width = tokens.shape
    top = expert_ids.shape[1]
    slots = experts * capacity
    return pl.pallas_call(
        lambda *refs: route_kernel(capacity, *refs),
        in_specs=[pl.BlockSpec(memory_space=pltpu.HBM)] * 4,
        out_specs=(VMEM_SPEC, VMEM_SPEC),
        out_shape=(
            jax.ShapeDtypeStruct((2 * slots, width), BF16),
            jax.ShapeDtypeStruct((tok, slots), BF16),
        ),
        scratch_shapes=[
            pltpu.VMEM((top, tok), jnp.int32),
            pltpu.VMEM((top, tok), F32),
            pltpu.VMEM((tok, width), BF16),
            pltpu.VMEM((tok, width), BF16),
            pltpu.VMEM((tok * top, width), BF16),
            pltpu.SemaphoreType.DMA((4,)),
        ],
        compiler_params=params(63),
        name="route",
    )(expert_ids.T, route_weights.T, tokens, out_grad)


def split_kernel(capacity, in_ref, out_ref):
    width = in_ref.shape[1]
    block = 32 * capacity
    rows = block // 2
    r = lax.broadcasted_iota(jnp.int32, (rows, block), 0)
    place = (r // capacity) * (2 * capacity) + r % capacity
    lane = lax.broadcasted_iota(jnp.int32, (rows, block), 1)
    for half in range(2):
        pick = (lane == place + half * capacity).astype(F32).astype(BF16)
        for b in range(in_ref.shape[0] // block):
            out_ref[b * rows : (b + 1) * rows, half * width : (half + 1) * width] = jnp.dot(
                pick, in_ref[b * block : (b + 1) * block, :], preferred_element_type=F32
            ).astype(BF16)


def split(received, capacity):
    rows, width = received.shape
    return pl.pallas_call(
        lambda *refs: split_kernel(capacity, *refs),
        in_specs=[VMEM_SPEC],
        out_specs=VMEM_SPEC,
        out_shape=jax.ShapeDtypeStruct((rows // 2, 2 * width), BF16),
        compiler_params=params(),
        name="split",
    )(received)


def chunk_start(me_ref, offset, n_rep, part):
    return pl.multiple_of(lax.rem(me_ref[0] + offset, n_rep) * part, part)


def chunk_weights(me_ref, offset, n_rep, wg_ref, wu_ref):
    part = wg_ref.shape[2] // n_rep
    cols = pl.ds(chunk_start(me_ref, offset, n_rep, part), part)
    return jnp.concatenate([wg_ref[0, :, cols], wu_ref[0, :, cols]], axis=1)


def term_kernel(offset, n_rep, me_ref, rows_ref, wg_ref, wu_ref, wd_ref, *refs):
    out_ref = refs[-1]
    width = wg_ref.shape[1]
    part = wg_ref.shape[2] // n_rep
    weights = chunk_weights(me_ref, offset, n_rep, wg_ref, wu_ref)
    down = wd_ref[0, pl.ds(chunk_start(me_ref, offset, n_rep, part), part), :]
    gate_up = jnp.dot(rows_ref[:, :width], weights, preferred_element_type=F32)
    hidden = lax.dot_general(rows_ref[:, width:], down, TRANS_B, preferred_element_type=F32)
    for arrived in refs[:-1]:
        gate_up = gate_up + arrived[:, : 2 * part].astype(F32)
        hidden = hidden + arrived[:, 2 * part :].astype(F32)
    out_ref[:, : 2 * part] = gate_up.astype(out_ref.dtype)
    out_ref[:, 2 * part :] = hidden.astype(out_ref.dtype)


def shift(rows, by):
    n_rep = lax.axis_size("rep")
    return lax.ppermute(rows, "rep", [(i, (i + by) % n_rep) for i in range(n_rep)])


def width_sums(me, both_rows, w_gate, w_up, w_down, n_rep):
    rows = both_rows.shape[0]
    part = w_gate.shape[2] // n_rep

    def term(offset, arrived, dtype, name):
        return pl.pallas_call(
            lambda *refs: term_kernel(offset, n_rep, *refs),
            in_specs=[pl.BlockSpec(memory_space=pltpu.SMEM)] + [VMEM_SPEC] * (4 + len(arrived)),
            out_specs=VMEM_SPEC,
            out_shape=jax.ShapeDtypeStruct((rows, 3 * part), dtype),
            compiler_params=params(),
            name=name,
        )(me, both_rows, w_gate, w_up, w_down, *arrived)

    half = n_rep // 2
    up, down = (), ()
    for hop in range(half, 0, -1):
        up = (shift(term(hop, up, BF16, "rise_%d" % hop), 1),)
        if hop < half:
            down = (shift(term(n_rep - hop, down, BF16, "fall_%d" % hop), -1),)
    return term(0, (), F32, "own_term"), up[0], down[0]


def activate_kernel(own_ref, up_ref, down_ref, out_ref):
    part = own_ref.shape[1] // 3
    sums = own_ref[...] + up_ref[...].astype(F32) + down_ref[...].astype(F32)
    gate = sums[:, :part]
    up = sums[:, part : 2 * part]
    hidden = sums[:, 2 * part :]
    s = jax.nn.sigmoid(gate)
    out_ref[:, :part] = (hidden * up * s * (1.0 + gate * (1.0 - s))).astype(BF16)
    out_ref[:, part:] = (hidden * gate * s).astype(BF16)


def activate(own, up, down):
    rows, part3 = own.shape
    return pl.pallas_call(
        activate_kernel,
        in_specs=[VMEM_SPEC] * 3,
        out_specs=VMEM_SPEC,
        out_shape=jax.ShapeDtypeStruct((rows, part3 // 3 * 2), BF16),
        compiler_params=params(),
        name="activate",
    )(own, up, down)


def row_grad_kernel(offsets, has_start, n_rep, me_ref, *refs):
    blocks = refs[: len(offsets)]
    wg_ref, wu_ref = refs[len(offsets) : len(offsets) + 2]
    out_ref = refs[-1]
    total = refs[-2][...] if has_start else None
    for offset, block in zip(offsets, blocks):
        weights = chunk_weights(me_ref, offset, n_rep, wg_ref, wu_ref)
        term = lax.dot_general(block[...], weights, TRANS_B, preferred_element_type=F32)
        total = term if total is None else total + term
    out_ref[...] = total.astype(out_ref.dtype)


def row_grad(me, blocks, offsets, w_gate, w_up, n_rep, start, dtype, name):
    rows = blocks[0].shape[0]
    width = w_gate.shape[1]
    extra = () if start is None else (start,)
    return pl.pallas_call(
        lambda *refs: row_grad_kernel(offsets, start is not None, n_rep, *refs),
        in_specs=[pl.BlockSpec(memory_space=pltpu.SMEM)]
        + [VMEM_SPEC] * (len(blocks) + 2 + len(extra)),
        out_specs=VMEM_SPEC,
        out_shape=jax.ShapeDtypeStruct((rows, width), dtype),
        compiler_params=params(),
        name=name,
    )(me, *blocks, w_gate, w_up, *extra)


def gather_matmul(me, own, w_gate, w_up, n_rep):
    half = n_rep // 2
    blocks, offsets = [own], [0]
    up = down = own
    for step in range(1, half):
        up, down = shift(up, 1), shift(down, -1)
        blocks += [up, down]
        offsets += [n_rep - step, step]
    last = shift(up, 1)
    total = row_grad(me, blocks, offsets, w_gate, w_up, n_rep, None, F32, "row_grad_near")
    return row_grad(me, [last], [half], w_gate, w_up, n_rep, total, BF16, "row_grad_far")


def combine_kernel(pt_ref, rows_ref, out_ref):
    total = jnp.dot(pt_ref[...], rows_ref[...], preferred_element_type=F32)
    out_ref[...] = total.astype(BF16)


def combine(per_token_t, returned):
    return pl.pallas_call(
        combine_kernel,
        in_specs=[VMEM_SPEC] * 2,
        out_specs=VMEM_SPEC,
        out_shape=jax.ShapeDtypeStruct((per_token_t.shape[0], returned.shape[1]), BF16),
        compiler_params=params(),
        name="combine",
    )(per_token_t, returned)


def per_device(tokens, out_grad, expert_ids, route_weights, gate_weight, up_weight, down_weight):
    tok, width = tokens.shape
    top = expert_ids.shape[1]
    n_rep = lax.axis_size("rep")
    experts = lax.axis_size("outer") * lax.axis_size("local")
    capacity = max(2, 2 * tok * top // experts)
    slots = experts * capacity
    me = lax.axis_index("rep").astype(jnp.int32).reshape(1)
    send, per_token_t = route(tokens, out_grad, expert_ids, route_weights, experts, capacity)

    def exchange(rows):
        blocks = rows.reshape(experts, rows.shape[0] // experts, width)
        return lax.all_to_all(blocks, ("outer", "local"), 0, 0, tiled=True).reshape(rows.shape)

    both_rows = split(exchange(send), capacity)
    own = activate(
        *width_sums(me, both_rows, gate_weight, up_weight, down_weight, n_rep)
    )
    returned = exchange(gather_matmul(me, own, gate_weight, up_weight, n_rep))
    return combine(per_token_t, returned)


def solution(mesh):
    return jax.shard_map(
        per_device,
        mesh=mesh,
        in_specs=(
            P(("outer", "local"), "rep"),
            P(("outer", "local"), "rep"),
            P(("outer", "local"), None),
            P(("outer", "local"), None),
            P(("outer", "local"), "rep", None),
            P(("outer", "local"), "rep", None),
            P(("outer", "local"), None, "rep"),
        ),
        out_specs=P(("outer", "local"), "rep"),
        check_vma=False,
    )
```
